32 devices in a mesh: section: 4 (over y, x), row: 8 (over z, core).
Axes of the slice: x: 2, y: 2, z: 4, core: 2. Of those that a mesh axis runs over, the one named last changes fastest.
Arguments:
- states: bfloat16 [4, 96, 768, 128], P('section', 'row'), may hold values from -6 to 6
- cotangent: bfloat16 [96, 768, 128], P('row'), may hold values from -6 to 6
- spec_weights: bfloat16 [64, 128, 2, 128, 128], P(None, 'row'), may hold values from -0.375 to 0.375
- local_weight: bfloat16 [128, 128], replicated, may hold values from -0.5 to 0.5
- bias: float32 [128], replicated, may hold values from -4 to 4
Outputs:
- grad_states: bfloat16 [4, 96, 768, 128], P('section', 'row')
- d_spectral: bfloat16 [64, 128, 2, 128, 128], P('section', 'row')
- d_local: float32 [128, 128], replicated
The draws below stay inside these ranges and needn't reach their ends.
All inputs are finite; a program needn't handle non-finite values.
Results may differ from the reference program's by a relative error of at most 0.017.
Values may be sent and summed in bfloat16 or wider, within the bound.
No kernel may reach another device: no remote copies, remote signals or barrier semaphores. Data moves between devices by JAX's collectives and lax.ppermute only.
A program may use at most 384 MiB of HBM per device.

```python
import math
import jax
import jax.numpy as jnp
from jax import lax

CHANNELS = 128
LAT_MODES = 64
LON_MODES = 128
LONGITUDE = 768
ROLLOUT = 4
LATITUDE = 96


def block_scale(stream_key, extent, cuts, smallest, top_value):
    gain, own = 1.0, jax.random.fold_in(stream_key, 6)
    for position, shards_of in cuts:
        steps = jnp.exp(jax.random.uniform(jax.random.fold_in(own, position), (shards_of,), jnp.float32, smallest / len(cuts), top_value / len(cuts)))
        gain = gain * jnp.repeat(steps, extent[position] // shards_of).reshape([-1 if axis == position else 1 for axis in range(len(extent))])
    return gain


def gaussian(rng, dims, deviation, limit, split=(), held_as=jnp.bfloat16):
    values = jax.random.normal(rng, dims, jnp.float32) * deviation
    if len(split) > 0:
        values = block_scale(rng, dims, split, -0.22, 0.18) * values
    return jnp.clip(values, min=-limit, max=limit).astype(held_as)


def setup_inputs(seed: int = 0) -> dict:
    key_list = jax.random.split(jax.random.key(seed), 6)
    states = gaussian(key_list[0], (ROLLOUT, LATITUDE, LONGITUDE, CHANNELS), 1.0, 6.0, ((0, 4), (1, 8)))
    cotangent = gaussian(key_list[1], (LATITUDE, LONGITUDE, CHANNELS), 1.0, 6.0, ((0, 8),))
    spec_weights = gaussian(key_list[2], (LAT_MODES, LON_MODES, 2, CHANNELS, CHANNELS), (2 * CHANNELS) ** -0.5, 0.375, ((1, 8),))
    local_weight = gaussian(key_list[3], (CHANNELS, CHANNELS), CHANNELS ** -0.5, 0.5)
    bias = gaussian(key_list[4], (CHANNELS,), 1.0, 4.0, (), jnp.float32)
    return {"states": states, "cotangent": cotangent, "spec_weights": spec_weights, "local_weight": local_weight, "bias": bias}


GELU_SLOPE = math.sqrt(2.0 / math.pi)
GELU_CUBIC = 0.044715

def gelu_derivative(values):
    inner_arg = GELU_SLOPE * (values + GELU_CUBIC * values * values * values)
    tangent = jnp.tanh(inner_arg)
    return 0.5 * (1.0 + tangent) + 0.5 * values * (1.0 - tangent * tangent) * GELU_SLOPE * (1.0 + 3.0 * GELU_CUBIC * values * values)

def lon_tables(mode_list, lon_cells):
    cell_ids = lax.iota(jnp.int32, lon_cells)
    phases = cell_ids[:, None] * mode_list[None, :] % lon_cells
    angles = phases.astype(jnp.float32) * (2.0 * math.pi / lon_cells)
    factor = 1.0 / math.sqrt(lon_cells)
    forward = jnp.stack([jnp.cos(angles), -jnp.sin(angles)], 2) * factor
    doubling = jnp.where(mode_list == 0, 1.0, 2.0).astype(jnp.float32)
    backward = jnp.transpose(forward, (1, 2, 0)) * doubling[:, None, None]
    return (forward.reshape(lon_cells, -1).astype(jnp.bfloat16), backward.reshape(-1, lon_cells).astype(jnp.bfloat16))

def lat_tables(row_list, freq_count, lat_cells):
    freq_index = lax.iota(jnp.int32, freq_count)
    signed = jnp.where(freq_index < freq_count // 2, freq_index, freq_index - freq_count)
    phases = (signed % lat_cells)[:, None] * row_list[None, :] % lat_cells
    angles = phases.astype(jnp.float32) * (2.0 * math.pi / lat_cells)
    factor = 1.0 / math.sqrt(lat_cells)
    return (jnp.stack([jnp.cos(angles), jnp.sin(angles)], 0) * factor).astype(jnp.bfloat16)

def lat_forward(values, tables):
    lat_cells, mode_count, pair_width = values.shape
    channels = pair_width // 2
    freq_count = tables.shape[1]
    paired = jnp.dot(tables.reshape(2 * freq_count, lat_cells), values.reshape(lat_cells, mode_count * pair_width), preferred_element_type=jnp.float32)
    paired = paired.reshape(2, freq_count, mode_count, 2, channels)
    real_part = paired[0, :, :, 0] + paired[1, :, :, 1]
    imag_part = paired[0, :, :, 1] - paired[1, :, :, 0]
    return jnp.stack([real_part, imag_part], 2).astype(jnp.bfloat16)

def lat_inverse(spectrum, tables):
    freq_count, mode_count, _, channels = spectrum.shape
    lat_cells = tables.shape[2]
    paired = jnp.einsum('tjh,jx->thx', tables.astype(jnp.float32), spectrum.reshape(freq_count, -1).astype(jnp.float32))
    paired = paired.reshape(2, lat_cells, mode_count, 2, channels)
    real_part = paired[0, :, :, 0] - paired[1, :, :, 1]
    imag_part = paired[0, :, :, 1] + paired[1, :, :, 0]
    return jnp.stack([real_part, imag_part], 2).reshape(lat_cells, mode_count, 2 * channels).astype(jnp.bfloat16)

def spectral(spectrum, spec_weights):

    def one_freq(pair_in):
        spec_row, weight_row = pair_in
        product = jnp.einsum('kpi,kqio->kpqo', spec_row.astype(jnp.float32), weight_row.astype(jnp.float32))
        real_part = product[:, 0, 0] - product[:, 1, 1]
        imag_part = product[:, 0, 1] + product[:, 1, 0]
        return jnp.stack([real_part, imag_part], 1).astype(jnp.bfloat16)
    return lax.map(one_freq, (spectrum, spec_weights))

def spectral_adjoint(cotan_spec, spec_weights):

    def one_freq(pair_in):
        cotan_row, weight_row = pair_in
        product = jnp.einsum('kqio,kpo->kqpi', weight_row.astype(jnp.float32), cotan_row.astype(jnp.float32))
        real_part = product[:, 0, 0] + product[:, 1, 1]
        imag_part = product[:, 0, 1] - product[:, 1, 0]
        return jnp.stack([real_part, imag_part], 1).astype(jnp.bfloat16)
    return lax.map(one_freq, (cotan_spec, spec_weights))

def weight_gradient(coeff_steps, cotan_steps):

    def one_freq(pair_in):
        coeff_row, cotan_row = pair_in
        product = jnp.einsum('skpi,skqo->kpqio', coeff_row.astype(jnp.float32), cotan_row.astype(jnp.float32))
        real_part = product[:, 0, 0] + product[:, 1, 1]
        imag_part = product[:, 0, 1] - product[:, 1, 0]
        return jnp.stack([real_part, imag_part], 1).astype(jnp.bfloat16)
    return lax.map(one_freq, (jnp.swapaxes(coeff_steps, 0, 1), jnp.swapaxes(cotan_steps, 0, 1)))

def forward_step(fields, spec_weights, local_weight, bias, lon_basis, lon_synth, lat_basis):
    row_count, lon_cells, channels = fields.shape
    mode_count = lon_basis.shape[1] // 2
    spectra = jnp.einsum('hwc,wm->hmc', fields.astype(jnp.float32), lon_basis.astype(jnp.float32)).astype(jnp.bfloat16)
    coefficients = lat_forward(spectra.reshape(row_count, mode_count, 2 * channels), lat_basis)
    mixed = spectral(coefficients, spec_weights)
    returned = lat_inverse(mixed, lat_basis)
    smooth = jnp.einsum('hmc,mw->hwc', returned.reshape(row_count, 2 * mode_count, channels).astype(jnp.float32), lon_synth.astype(jnp.float32))
    linear = jnp.dot(fields.reshape(-1, channels), local_weight, preferred_element_type=jnp.float32).reshape(row_count, lon_cells, channels)
    return (smooth + linear + bias, coefficients)

def backward_step(fields, pre_act, carried, spec_weights, local_weight, lon_basis, lon_synth, lat_basis):
    row_count, lon_cells, channels = fields.shape
    mode_count = lon_basis.shape[1] // 2
    slopes = carried.astype(jnp.float32) * gelu_derivative(pre_act)
    slopes_low = slopes.astype(jnp.bfloat16)
    spectra = jnp.einsum('hwc,mw->hmc', slopes_low.astype(jnp.float32), lon_synth.astype(jnp.float32)).astype(jnp.bfloat16)
    coeff_cotan = lat_forward(spectra.reshape(row_count, mode_count, 2 * channels), lat_basis)
    inner_cotan = spectral_adjoint(coeff_cotan, spec_weights)
    returned = lat_inverse(inner_cotan, lat_basis)
    spread = jnp.einsum('hmc,wm->hwc', returned.reshape(row_count, 2 * mode_count, channels).astype(jnp.float32), lon_basis.astype(jnp.float32))
    flat_slopes = slopes_low.reshape(-1, channels)
    linear = lax.dot_general(flat_slopes, local_weight, (((1,), (1,)), ((), ())), preferred_element_type=jnp.float32)
    gradient = (carried.astype(jnp.float32) + linear.reshape(row_count, lon_cells, channels) + spread).astype(jnp.bfloat16)
    step_term = lax.dot_general(fields.reshape(-1, channels), flat_slopes, (((0,), (0,)), ((), ())), preferred_element_type=jnp.float32)
    return (gradient, coeff_cotan, step_term)

def reference(states, cotangent, spec_weights, local_weight, bias):
    lon_basis, lon_synth = lon_tables(lax.iota(jnp.int32, LON_MODES), LONGITUDE)
    lat_basis = lat_tables(lax.iota(jnp.int32, LATITUDE), LAT_MODES, LATITUDE)
    carried = cotangent
    grad_list = [None] * ROLLOUT
    coeff_list = [None] * ROLLOUT
    cotan_list = [None] * ROLLOUT
    local_sum = jnp.zeros((CHANNELS, CHANNELS), jnp.float32)
    for step_no in range(ROLLOUT - 1, -1, -1):
        pre_act, coefficients = forward_step(states[step_no], spec_weights, local_weight, bias, lon_basis, lon_synth, lat_basis)
        carried, coeff_cotan, step_term = backward_step(states[step_no], pre_act, carried, spec_weights, local_weight, lon_basis, lon_synth, lat_basis)
        grad_list[step_no] = carried
        coeff_list[step_no] = coefficients
        cotan_list[step_no] = coeff_cotan
        local_sum = local_sum + step_term
    d_spectral = weight_gradient(jnp.stack(coeff_list, 0), jnp.stack(cotan_list, 0))
    d_local = local_sum * lax.rsqrt(jnp.float32(ROLLOUT * LATITUDE * LONGITUDE))
    return (jnp.stack(grad_list, 0), d_spectral, d_local)
```

```python
import functools
import math

import jax
import jax.numpy as jnp
import numpy as np
from jax import lax
from jax.experimental import pallas as pl
from jax.experimental.pallas import tpu as pltpu
from jax.sharding import PartitionSpec as P

GELU_SLOPE = math.sqrt(2.0 / math.pi)
GELU_CUBIC = 0.044715
BF16 = jnp.bfloat16
F32 = jnp.float32
ALL = ("section", "row")
VMEM_LIMIT = 56 * 1024 * 1024


def gelu_derivative(values):
    square = values * values
    inner_arg = GELU_SLOPE * values * (1.0 + GELU_CUBIC * square)
    tangent = jnp.tanh(inner_arg)
    return 0.5 * (1.0 + tangent) + (0.5 * GELU_SLOPE) * values * (1.0 - tangent * tangent) * (
        1.0 + 3.0 * GELU_CUBIC * square
    )


def lon_tables(mode_list, lon_cells):
    phases = np.arange(lon_cells)[:, None] * mode_list[None, :] % lon_cells
    angles = phases * (2.0 * math.pi / lon_cells)
    factor = 1.0 / math.sqrt(lon_cells)
    forward = np.stack([np.cos(angles), -np.sin(angles)], 2) * factor
    doubling = np.where(mode_list == 0, 1.0, 2.0)
    backward = np.transpose(forward, (1, 2, 0)) * doubling[:, None, None]
    return (
        forward.reshape(lon_cells, -1).astype(np.float32),
        backward.reshape(-1, lon_cells).astype(np.float32),
    )


def lat_matrices(row_list, freq_count, lat_cells, modes):
    freq = np.arange(freq_count)
    signed = np.where(freq < freq_count // 2, freq, freq - freq_count)
    angles = ((signed % lat_cells)[:, None] * row_list[None, :] % lat_cells) * (
        2.0 * math.pi / lat_cells
    )
    factor = 1.0 / math.sqrt(lat_cells)
    cos, sin = np.cos(angles) * factor, np.sin(angles) * factor
    same = np.eye(modes)
    rot = np.array([[[1.0, 0.0], [0.0, 1.0]], [[0.0, 1.0], [-1.0, 0.0]]])
    block = cos[:, None, None, :, None, None] * same[None, :, None, None, :, None] * rot[0][
        None, None, :, None, None, :
    ] + sin[:, None, None, :, None, None] * same[None, :, None, None, :, None] * rot[1][
        None, None, :, None, None, :
    ]
    return block.reshape(freq_count * modes * 2, row_list.size * modes * 2).astype(np.float32)


def dot(a, b, contract=((1,), (0,))):
    return lax.dot_general(a, b, (contract, ((), ())), preferred_element_type=F32)


def unpack_rows(values, rows, packed):
    channels = values.shape[-1]
    if packed:
        devices, per_dev, _ = values.shape
        wide = values.astype(F32).reshape(devices, per_dev // 8, 8, channels)
        parts = [wide[:, r].reshape(devices * 8, channels) for r in rows]
    else:
        parts = [values[r].astype(F32) for r in rows]
    return jnp.concatenate(parts, axis=1).astype(BF16)


def pack_rows(spec, row_count, packed, devices):
    channels = spec.shape[1] // row_count
    parts = [spec[:, r * channels : (r + 1) * channels] for r in range(row_count)]
    if packed:
        parts = [p.reshape(devices, 8, channels) for p in parts]
        return jnp.concatenate(parts, axis=1).astype(BF16)
    return jnp.stack(parts, 0).astype(BF16)


def outer_pack(spec, devices):
    rows, total, channels = spec.shape
    per = total // devices
    return spec.reshape(rows, devices, per, channels).transpose(1, 0, 2, 3).reshape(
        devices, rows * per, channels
    )


def outer_unpack(received, row_count):
    devices, total, channels = received.shape
    per = total // row_count
    return received.reshape(devices, row_count, per, channels).transpose(1, 0, 2, 3).reshape(
        row_count, devices * per, channels
    )


def spectra_kernel(rows_at_once, packed, devices, fields_ref, basis_ref, out_ref):
    basis = basis_ref[...]
    row_count = fields_ref.shape[0]
    for first in range(0, row_count, rows_at_once):
        field = jnp.concatenate([fields_ref[first + r] for r in range(rows_at_once)], axis=1)
        spec = pack_rows(dot(basis, field), rows_at_once, packed, devices)
        if packed:
            out_ref[:, first * 8 : (first + rows_at_once) * 8, :] = spec
        else:
            out_ref[first : first + rows_at_once] = spec


def spread_pairs(values, per_group, sign):
    rows, _ = values.shape
    ids = lax.broadcasted_iota(jnp.int32, values.shape, 0)
    after = pltpu.roll(values, rows - 1, 0)
    before = pltpu.roll(values, 1, 0)
    turned = jnp.where(ids % 2 == 0, sign * after, -sign * before)
    pair = (ids // 2) % per_group
    parts = []
    for t in range(per_group):
        parts.append(jnp.where(pair == t, values, 0.0).astype(BF16))
        parts.append(jnp.where(pair == t, turned, 0.0).astype(BF16))
    return parts


def mix_kernel(steps, sec_ref, x_ref, lat_ref, inv_ref, w_ref, coeff_ref, out_ref, lhs_ref, z_ref):
    turn = pl.program_id(0)
    channels = x_ref.shape[-1]
    span = x_ref.shape[0] // steps
    total = lat_ref.shape[0]
    groups = total // 8

    @pl.when(turn == 0)
    def _():
        lat = lat_ref[...]
        found = []
        for s in range(steps):
            value = dot(lat, x_ref[s * span : (s + 1) * span, :]).astype(BF16)
            coeff_ref[s] = value
            found.append(value.astype(F32).reshape(groups, 8, channels))
        tall = jnp.concatenate(found, axis=1).reshape(groups * steps * 8, channels)
        for n, part in enumerate(spread_pairs_steps(tall, steps)):
            lhs_ref[:, n * channels : (n + 1) * channels] = part

    pairs = w_ref.shape[0] * w_ref.shape[1]
    here = pairs // 4
    weights = w_ref[...].reshape(here, 8 * channels, channels)
    for g in range(here):
        at = pl.multiple_of((turn * here + g) * (8 * steps), 8 * steps)
        mixed = dot(lhs_ref[pl.ds(at, 8 * steps), :], weights[g])
        to = pl.multiple_of((turn * here + g) * 8, 8)
        for s in range(steps):
            z_ref[s, pl.ds(to, 8), :] = mixed[s * 8 : (s + 1) * 8]

    @pl.when(turn == pl.num_programs(0) - 1)
    def _():
        inv = inv_ref[...]
        for s in range(steps):
            out_ref[s] = dot(inv, z_ref[s].astype(BF16)).astype(BF16)


def spread_pairs_steps(values, steps):
    return spread_pairs(values, 4, -1.0)


def adjoint_kernel(sec_ref, x_ref, lat_ref, inv_ref, w_ref, coeff_ref, out_ref, lhs_ref, z_ref):
    turn = pl.program_id(0)
    channels = x_ref.shape[-1]

    @pl.when(turn == 0)
    def _():
        value = dot(lat_ref[...], x_ref[...]).astype(BF16)
        coeff_ref[...] = value
        for n, part in enumerate(spread_pairs(value.astype(F32), 8, 1.0)):
            lhs_ref[:, n * channels : (n + 1) * channels] = part

    pairs = w_ref.shape[0] * w_ref.shape[1]
    here = pairs // 8
    weights = w_ref[...].reshape(here, 8, 2, channels, channels)
    for g in range(here):
        at = pl.multiple_of((turn * here + g) * 16, 16)
        mixed = jnp.zeros((16, channels), F32)
        for t in range(8):
            left = lhs_ref[pl.ds(at, 16), 2 * t * channels : (2 * t + 2) * channels]
            right = jnp.concatenate([weights[g, t, 0], weights[g, t, 1]], axis=1)
            mixed = mixed + dot(left, right, ((1,), (1,)))
        z_ref[pl.ds(at, 16), :] = mixed

    @pl.when(turn == pl.num_programs(0) - 1)
    def _():
        out_ref[...] = dot(inv_ref[...], z_ref[...].astype(BF16)).astype(BF16)


def slope_kernel(
    step, rows, packed, sec_ref, recv_ref, state_ref, synth_ref, mix_ref, bias_ref, out_ref
):
    channels = mix_ref.shape[0]
    cells = state_ref.shape[2]
    modes = unpack_rows(recv_ref[...], range(step * rows, (step + 1) * rows), packed)
    mixing = mix_ref[...]
    bias = bias_ref[...]
    tile = 256
    for w in range(0, cells, tile):
        smooth = dot(synth_ref[w : w + tile, :], modes)
        for r in range(rows):
            linear = dot(state_ref[0, r, w : w + tile, :], mixing)
            pre = smooth[:, r * channels : (r + 1) * channels] + linear + bias
            out_ref[r, w : w + tile, :] = gelu_derivative(pre)


def finish_tile(
    r, w, tile, carried, slope_ref, state_ref, low_ref
):
    low = (carried.astype(F32) * slope_ref[r, w : w + tile, :]).astype(BF16)
    low_ref[r, w : w + tile, :] = low
    term = dot(state_ref[0, r, w : w + tile, :], low, ((0,), (0,)))
    return low, term


def start_kernel(
    packed, devices, sec_ref, cot_ref, slope_ref, state_ref, synth_ref, low_ref, send_ref, acc_ref
):
    rows, cells, channels = cot_ref.shape
    tile = 256
    spec, acc = None, None
    for w in range(0, cells, tile):
        lows = []
        for r in range(rows):
            low, term = finish_tile(
                r, w, tile, cot_ref[r, w : w + tile, :], slope_ref, state_ref, low_ref
            )
            lows.append(low)
            acc = term if acc is None else acc + term
        part = dot(synth_ref[:, w : w + tile], jnp.concatenate(lows, axis=1))
        spec = part if spec is None else spec + part
    acc_ref[...] = acc
    send_ref[...] = pack_rows(spec, rows, packed, devices)


def gradient_tile(r, w, tile, spread, carried_ref, low_ref, mixing):
    channels = mixing.shape[0]
    linear = dot(low_ref[r, w : w + tile, :], mixing, ((1,), (1,)))
    total = (
        carried_ref[r, w : w + tile, :].astype(F32)
        + linear
        + spread[:, r * channels : (r + 1) * channels]
    )
    return total.astype(BF16)


def turn_kernel(
    packed,
    devices,
    sec_ref,
    recv_ref,
    carried_ref,
    prev_ref,
    slope_ref,
    state_ref,
    basis_ref,
    synth_ref,
    mix_ref,
    acc_in_ref,
    grad_ref,
    low_ref,
    send_ref,
    acc_ref,
):
    rows, cells, channels = carried_ref.shape
    modes = unpack_rows(recv_ref[...], range(rows), packed)
    mixing = mix_ref[...]
    tile = 256
    spec, acc = None, acc_in_ref[...]
    for w in range(0, cells, tile):
        spread = dot(basis_ref[w : w + tile, :], modes)
        lows = []
        for r in range(rows):
            grad = gradient_tile(r, w, tile, spread, carried_ref, prev_ref, mixing)
            grad_ref[r, w : w + tile, :] = grad
            low, term = finish_tile(r, w, tile, grad, slope_ref, state_ref, low_ref)
            lows.append(low)
            acc = acc + term
        part = dot(synth_ref[:, w : w + tile], jnp.concatenate(lows, axis=1))
        spec = part if spec is None else spec + part
    acc_ref[...] = acc
    send_ref[...] = pack_rows(spec, rows, packed, devices)


def last_kernel(packed, recv_ref, carried_ref, prev_ref, basis_ref, mix_ref, grad_ref):
    rows, cells, channels = carried_ref.shape
    modes = unpack_rows(recv_ref[...], range(rows), packed)
    mixing = mix_ref[...]
    tile = 256
    for w in range(0, cells, tile):
        spread = dot(basis_ref[w : w + tile, :], modes)
        for r in range(rows):
            grad_ref[r, w : w + tile, :] = gradient_tile(
                r, w, tile, spread, carried_ref, prev_ref, mixing
            )


def weight_kernel(steps, *refs):
    coeff_ref, cot_refs, out_ref = refs[0], refs[1 : 1 + steps], refs[1 + steps]
    channels = out_ref.shape[-1]
    tall = coeff_ref.shape[2]
    groups = tall // 8
    left = jnp.concatenate(
        [coeff_ref[s, 0].astype(F32).reshape(groups, 8, channels) for s in range(steps)], axis=1
    )
    right = jnp.concatenate(
        [ref[0].astype(F32).reshape(groups, 8, channels) for ref in cot_refs], axis=1
    )
    span = steps * 8
    left = left.reshape(groups * span, channels)
    right = right.reshape(groups * span, channels)
    ids = lax.broadcasted_iota(jnp.int32, right.shape, 0)
    turned = jnp.where(
        ids % 2 == 0,
        pltpu.roll(right, groups * span - 1, 0),
        -pltpu.roll(right, 1, 0),
    )
    right = jnp.concatenate([right, turned], axis=1).astype(BF16)
    pair = (ids // 2) % 4
    lefts = [jnp.where(pair == t, left, 0.0).astype(BF16) for t in range(4)]
    per_j = out_ref.shape[1]
    for g in range(groups):
        rhs = right[g * span : (g + 1) * span]
        for t in range(4):
            product = dot(lefts[t][g * span : (g + 1) * span], rhs, ((0,), (0,))).astype(BF16)
            j, k = divmod(g * 4 + t, per_j)
            out_ref[j, k, 0] = product[:, :channels]
            out_ref[j, k, 1] = product[:, channels:]


def whole(shape):
    return pl.BlockSpec(shape, lambda *_: (0,) * len(shape))


def call(kernel, outs, in_specs, operands, grid=(1,), out_specs=None, scratch=(), prefetch=None,
         flops=0, moved=0):
    if out_specs is None:
        out_specs = [whole(o.shape) for o in outs]
    count = 0 if prefetch is None else 1
    lead = () if prefetch is None else (prefetch,)
    return pl.pallas_call(
        kernel,
        out_shape=outs,
        grid_spec=pltpu.PrefetchScalarGridSpec(
            num_scalar_prefetch=count,
            grid=grid,
            in_specs=in_specs,
            out_specs=out_specs,
            scratch_shapes=list(scratch),
        ),
        compiler_params=pltpu.CompilerParams(
            vmem_limit_bytes=VMEM_LIMIT, dimension_semantics=("arbitrary",) * len(grid)
        ),
        cost_estimate=pl.CostEstimate(flops=flops, bytes_accessed=moved, transcendentals=0),
    )(*lead, *operands)


def local(states, cotangent, spec_weights, local_weight, bias):
    sections = lax.axis_size("section")
    row_devs = lax.axis_size("row")
    section = lax.axis_index("section")
    devices = sections * row_devs
    channels = local_weight.shape[0]
    cells = states.shape[2]
    rows_here = states.shape[1]
    rows = rows_here // sections
    freqs = spec_weights.shape[0]
    row_modes = spec_weights.shape[1]
    modes = row_modes // sections
    parts = 2 * modes
    lat_cells = rows_here * row_devs
    packed = parts == 8
    sec = section.astype(jnp.int32).reshape(1)

    order = (
        np.arange(row_devs)[None, :, None] * row_modes
        + np.arange(sections)[:, None, None] * modes
        + np.arange(modes)[None, None, :]
    ).reshape(-1)
    basis_np, synth_np = lon_tables(order, cells)
    basis = jnp.asarray(basis_np, BF16)
    basis_t = jnp.asarray(basis_np.T, BF16)
    synth = jnp.asarray(synth_np, BF16)
    synth_t = jnp.asarray(synth_np.T, BF16)
    row_order = (
        np.arange(row_devs)[None, :, None] * rows_here
        + np.arange(sections)[:, None, None] * rows
        + np.arange(rows)[None, None, :]
    ).reshape(-1)
    lat_plain = jnp.asarray(lat_matrices(np.arange(lat_cells), freqs, lat_cells, modes), BF16)
    shared_np = lat_matrices(row_order, freqs, lat_cells, modes)
    lat_shared = jnp.asarray(shared_np, BF16)
    inv_shared = jnp.asarray(shared_np.T, BF16)
    mode_rows = lat_plain.shape[0]
    grid_rows = lat_plain.shape[1]

    def exchange(values):
        return lax.all_to_all(values, ALL, 0, 0, tiled=True)

    own = states[0].reshape(sections, rows, cells, channels)
    pieces = [lax.dynamic_index_in_dim(own, section, 0, False)]
    for d in range(1, sections):
        piece = lax.dynamic_index_in_dim(own, section ^ d, 0, False)
        pieces.append(lax.ppermute(piece, "section", [(i, i ^ d) for i in range(sections)]))
    all_states = jnp.stack(pieces, 0)

    total = basis_t.shape[0]
    out_shape = (devices, rows_here * 8, channels) if packed else (rows_here, total, channels)
    (spectra,) = call(
        functools.partial(spectra_kernel, 2, packed, devices),
        [jax.ShapeDtypeStruct(out_shape, BF16)],
        [whole(states.shape[1:]), whole(basis_t.shape)],
        (states[0], basis_t),
        flops=2 * total * cells * rows_here * channels,
        moved=4 * rows_here * cells * channels,
    )
    if not packed:
        spectra = outer_pack(spectra, devices)
    gathered = exchange(spectra).reshape(sections * grid_rows, channels)

    block_j = max(1, min(freqs, 32 // modes))
    weight_block = (block_j, modes, 2, channels, channels)
    weight_spec = pl.BlockSpec(weight_block, lambda b, s: (b, s[0], 0, 0, 0))
    weight_bytes = 4 * freqs * modes * channels * channels
    coeffs, mixed = call(
        functools.partial(mix_kernel, sections),
        [
            jax.ShapeDtypeStruct((sections, mode_rows, channels), BF16),
            jax.ShapeDtypeStruct((sections, grid_rows, channels), BF16),
        ],
        [whole(gathered.shape), whole(lat_plain.shape), whole(inv_shared.shape), weight_spec],
        (gathered, lat_plain, inv_shared, spec_weights),
        grid=(freqs // block_j,),
        scratch=[
            pltpu.VMEM((sections * mode_rows, 8 * channels), BF16),
            pltpu.VMEM((sections, mode_rows, channels), F32),
        ],
        prefetch=sec,
        flops=4 * weight_bytes,
        moved=weight_bytes,
    )
    mixed = mixed.reshape(sections, devices, rows * parts, channels).transpose(1, 0, 2, 3)
    back = exchange(mixed.reshape(devices, sections * rows * parts, channels))
    if not packed:
        back = outer_unpack(back, sections * rows)

    field_block = (1, rows, cells, channels)
    shape3 = (rows, cells, channels)
    bias2 = bias.reshape(1, channels)
    slopes = [None] * sections
    for s in range(sections - 1, -1, -1):
        (slopes[s],) = call(
            functools.partial(slope_kernel, s, rows, packed),
            [jax.ShapeDtypeStruct(shape3, F32)],
            [
                whole(back.shape),
                pl.BlockSpec(field_block, functools.partial(lambda s, b, i: (i[0] ^ s, 0, 0, 0), s)),
                whole(synth_t.shape),
                whole(local_weight.shape),
                whole(bias2.shape),
            ],
            (back, all_states, synth_t, local_weight, bias2),
            prefetch=sec,
            flops=2 * total * cells * rows * channels,
            moved=10 * rows * cells * channels,
        )

    send_shape = (devices, rows * 8, channels) if packed else (rows, total, channels)
    turn_outs = [
        jax.ShapeDtypeStruct(shape3, BF16),
        jax.ShapeDtypeStruct(send_shape, BF16),
        jax.ShapeDtypeStruct((channels, channels), F32),
    ]

    def state_spec(s):
        return pl.BlockSpec(field_block, lambda b, i: (i[0] ^ s, 0, 0, 0))

    s = sections - 1
    carried = lax.dynamic_slice_in_dim(cotangent, section * rows, rows, 0)
    low, send, acc = call(
        functools.partial(start_kernel, packed, devices),
        turn_outs,
        [whole(shape3), whole(shape3), state_spec(s), whole(synth.shape)],
        (carried, slopes[s], all_states, synth),
        prefetch=sec,
        flops=2 * total * cells * rows * channels,
        moved=10 * rows * cells * channels,
    )
    grads = [None] * sections
    cots = [None] * sections
    slot = -(-channels // devices)
    for s in range(sections - 1, -1, -1):
        if not packed:
            send = outer_pack(send, devices)
        if s == 0:
            terms = jnp.pad(acc, ((0, slot * devices - channels), (0, 0)))
            terms = terms.reshape(devices, slot, channels)
            high = terms.astype(BF16)
            rest = (terms - high.astype(F32)).astype(BF16)
            send = jnp.concatenate([send, high, rest], axis=1)
        got = exchange(send)
        if s == 0:
            sums = jnp.sum(got[:, rows * parts :].astype(F32), 0)
            sums = sums[:slot] + sums[slot:]
            got = got[:, : rows * parts]
        cots[s], inner = call(
            adjoint_kernel,
            [
                jax.ShapeDtypeStruct((mode_rows, channels), BF16),
                jax.ShapeDtypeStruct((grid_rows, channels), BF16),
            ],
            [
                whole((grid_rows, channels)),
                whole(lat_shared.shape),
                whole(inv_shared.shape),
                weight_spec,
            ],
            (got.reshape(grid_rows, channels), lat_shared, inv_shared, spec_weights),
            grid=(freqs // block_j,),
            scratch=[
                pltpu.VMEM((mode_rows, 16 * channels), BF16),
                pltpu.VMEM((mode_rows, channels), F32),
            ],
            prefetch=sec,
            flops=2 * weight_bytes,
            moved=weight_bytes,
        )
        inner = inner.reshape(devices, rows * parts, channels)
        if s == 0:
            high = sums.astype(BF16)
            rest = (sums - high.astype(F32)).astype(BF16)
            both = jnp.concatenate([high, rest], 0)
            both = jnp.broadcast_to(both[None], (devices,) + both.shape)
            inner = jnp.concatenate([inner, both], axis=1)
        got = exchange(inner)
        if s == 0:
            both = got[:, rows * parts :].astype(F32)
            got = got[:, : rows * parts]
            local_total = (both[:, :slot] + both[:, slot:]).reshape(-1, channels)[:channels]
        if not packed:
            got = outer_unpack(got, rows)
        if s > 0:
            grads[s], low, send, acc = call(
                functools.partial(turn_kernel, packed, devices),
                [jax.ShapeDtypeStruct(shape3, BF16)] + turn_outs,
                [
                    whole(got.shape),
                    whole(shape3),
                    whole(shape3),
                    whole(shape3),
                    state_spec(s - 1),
                    whole(basis.shape),
                    whole(synth.shape),
                    whole(local_weight.shape),
                    whole(acc.shape),
                ],
                (got, carried, low, slopes[s - 1], all_states, basis, synth, local_weight, acc),
                prefetch=sec,
                flops=4 * total * cells * rows * channels,
                moved=16 * rows * cells * channels,
            )
            carried = grads[s]
        else:
            (grads[0],) = call(
                functools.partial(last_kernel, packed),
                [jax.ShapeDtypeStruct(shape3, BF16)],
                [
                    whole(got.shape),
                    whole(shape3),
                    whole(shape3),
                    whole(basis.shape),
                    whole(local_weight.shape),
                ],
                (got, carried, low, basis, local_weight),
                flops=2 * total * cells * rows * channels,
                moved=8 * rows * cells * channels,
            )

    d_local = local_total * lax.rsqrt(jnp.float32(sections * lat_cells * cells))

    part = mode_rows // sections

    def to_sections(values, axis):
        return lax.all_to_all(values, "section", axis, axis, tiled=True)

    step_coeffs = to_sections(coeffs.reshape(sections, sections, part, channels), 1)
    step_cots = [to_sections(c.reshape(sections, part, channels), 0) for c in cots]
    own_freqs = freqs // sections
    own_j = max(1, min(own_freqs, 32 // modes))
    tall = own_j * parts
    (d_spectral,) = call(
        functools.partial(weight_kernel, sections),
        [jax.ShapeDtypeStruct((own_freqs, row_modes, 2, channels, channels), BF16)],
        [pl.BlockSpec((sections, 1, tall, channels), lambda a, b: (0, a, b, 0))]
        + [pl.BlockSpec((1, tall, channels), lambda a, b: (a, b, 0))] * sections,
        (step_coeffs, *step_cots),
        grid=(sections, own_freqs // own_j),
        out_specs=[
            pl.BlockSpec((own_j, modes, 2, channels, channels), lambda a, b: (b, a, 0, 0, 0))
        ],
        flops=8 * weight_bytes,
        moved=weight_bytes,
    )

    grad_states = lax.all_to_all(jnp.stack(grads, 0), "section", 0, 0, tiled=True)
    grad_states = grad_states.reshape(1, rows_here, cells, channels)
    return (grad_states, d_spectral, d_local)


def solution(mesh):
    return jax.shard_map(
        local,
        mesh=mesh,
        in_specs=(
            P("section", "row", None, None),
            P("row", None, None),
            P(None, "row", None, None, None),
            P(),
            P(),
        ),
        out_specs=(P("section", "row", None, None), P("section", "row", None, None, None), P()),
        check_vma=False,
    )
```

```python
import functools
import math

import jax
import jax.numpy as jnp
import numpy as np
from jax import lax
from jax.experimental import pallas as pl
from jax.experimental.pallas import tpu as pltpu
from jax.sharding import PartitionSpec as P

GELU_SLOPE = math.sqrt(2.0 / math.pi)
GELU_CUBIC = 0.044715
BF16 = jnp.bfloat16
F32 = jnp.float32
ALL = ("section", "row")
VMEM_LIMIT = 56 * 1024 * 1024
CHUNK = 16


def gelu_derivative(values):
    square = values * values
    inner_arg = GELU_SLOPE * values * (1.0 + GELU_CUBIC * square)
    tangent = jnp.tanh(inner_arg)
    return 0.5 * (1.0 + tangent) + (0.5 * GELU_SLOPE) * values * (1.0 - tangent * tangent) * (
        1.0 + 3.0 * GELU_CUBIC * square
    )


def lon_tables(mode_list, lon_cells):
    phases = np.arange(lon_cells)[:, None] * mode_list[None, :] % lon_cells
    angles = phases * (2.0 * math.pi / lon_cells)
    factor = 1.0 / math.sqrt(lon_cells)
    forward = np.stack([np.cos(angles), -np.sin(angles)], 2) * factor
    doubling = np.where(mode_list == 0, 1.0, 2.0)
    backward = np.transpose(forward, (1, 2, 0)) * doubling[:, None, None]
    return (
        forward.reshape(lon_cells, -1).astype(np.float32),
        backward.reshape(-1, lon_cells).astype(np.float32),
    )


def lat_matrices(row_list, freq_count, lat_cells, modes):
    freq = np.arange(freq_count)
    signed = np.where(freq < freq_count // 2, freq, freq - freq_count)
    angles = ((signed % lat_cells)[:, None] * row_list[None, :] % lat_cells) * (
        2.0 * math.pi / lat_cells
    )
    factor = 1.0 / math.sqrt(lat_cells)
    cos, sin = np.cos(angles) * factor, np.sin(angles) * factor
    same = np.eye(modes)
    rot = np.array([[[1.0, 0.0], [0.0, 1.0]], [[0.0, 1.0], [-1.0, 0.0]]])
    block = cos[:, None, None, :, None, None] * same[None, :, None, None, :, None] * rot[0][
        None, None, :, None, None, :
    ] + sin[:, None, None, :, None, None] * same[None, :, None, None, :, None] * rot[1][
        None, None, :, None, None, :
    ]
    return block.reshape(freq_count * modes * 2, row_list.size * modes * 2).astype(np.float32)


def dot(a, b, contract=((1,), (0,))):
    return lax.dot_general(a, b, (contract, ((), ())), preferred_element_type=F32)


def unpack_rows(values, rows, packed):
    channels = values.shape[-1]
    if packed:
        devices, per_dev, _ = values.shape
        wide = values.astype(F32).reshape(devices, per_dev // 8, 8, channels)
        parts = [wide[:, r].reshape(devices * 8, channels) for r in rows]
    else:
        parts = [values[r].astype(F32) for r in rows]
    return jnp.concatenate(parts, axis=1).astype(BF16)


def pack_rows(spec, row_count, packed, devices):
    channels = spec.shape[1] // row_count
    parts = [spec[:, r * channels : (r + 1) * channels] for r in range(row_count)]
    if packed:
        parts = [p.reshape(devices, 8, channels) for p in parts]
        return jnp.concatenate(parts, axis=1).astype(BF16)
    return jnp.stack(parts, 0).astype(BF16)


def outer_pack(spec, devices):
    rows, total, channels = spec.shape
    per = total // devices
    return spec.reshape(rows, devices, per, channels).transpose(1, 0, 2, 3).reshape(
        devices, rows * per, channels
    )


def outer_unpack(received, row_count):
    devices, total, channels = received.shape
    per = total // row_count
    return received.reshape(devices, row_count, per, channels).transpose(1, 0, 2, 3).reshape(
        row_count, devices * per, channels
    )


def spectra_kernel(rows_at_once, packed, devices, fields_ref, basis_ref, out_ref):
    basis = basis_ref[...]
    row_count = fields_ref.shape[0]
    for first in range(0, row_count, rows_at_once):
        field = jnp.concatenate([fields_ref[first + r] for r in range(rows_at_once)], axis=1)
        spec = pack_rows(dot(basis, field), rows_at_once, packed, devices)
        if packed:
            out_ref[:, first * 8 : (first + rows_at_once) * 8, :] = spec
        else:
            out_ref[first : first + rows_at_once] = spec


def spread_pairs(values, per_group, sign):
    rows, _ = values.shape
    ids = lax.broadcasted_iota(jnp.int32, values.shape, 0)
    after = pltpu.roll(values, rows - 1, 0)
    before = pltpu.roll(values, 1, 0)
    turned = jnp.where(ids % 2 == 0, sign * after, -sign * before)
    pair = (ids // 2) % per_group
    parts = []
    for t in range(per_group):
        parts.append(jnp.where(pair == t, values, 0.0).astype(BF16))
        parts.append(jnp.where(pair == t, turned, 0.0).astype(BF16))
    return parts


def weight_copies(sec_ref, all_ref, weights_ref, sems):
    span = weights_ref.shape[0] // sems.shape[0]
    modes = weights_ref.shape[1]
    first = sec_ref[0] * modes

    def chunk(n):
        return pltpu.make_async_copy(
            all_ref.at[pl.ds(n * span, span), pl.ds(first, modes)],
            weights_ref.at[pl.ds(n * span, span)],
            sems.at[n],
        )

    for n in range(sems.shape[0]):
        chunk(n).start()
    return chunk


def mix_kernel(
    steps, packed, sec_ref, x_ref, lat_ref, inv_ref, all_ref, coeff_ref, out_ref, weights_ref,
    lhs_ref, z_ref, sems
):
    chunk = weight_copies(sec_ref, all_ref, weights_ref, sems)
    channels = x_ref.shape[-1]
    span = x_ref.shape[0] // steps
    groups = lat_ref.shape[0] // 8
    lat = lat_ref[...]
    found = []
    for s in range(steps):
        value = dot(lat, x_ref[s * span : (s + 1) * span, :]).astype(BF16)
        coeff_ref[s] = value
        found.append(value.astype(F32).reshape(groups, 8, channels))
    tall = jnp.concatenate(found, axis=1).reshape(groups * steps * 8, channels)
    for n, part in enumerate(spread_pairs(tall, 4, -1.0)):
        lhs_ref[:, n * channels : (n + 1) * channels] = part

    block = weights_ref.shape[0] // sems.shape[0]
    per_chunk = groups // sems.shape[0]

    @pl.loop(0, sems.shape[0])
    def _(n):
        chunk(n).wait()
        here = weights_ref[pl.ds(n * block, block)].reshape(per_chunk, 8 * channels, channels)
        for g in range(per_chunk):
            at = pl.multiple_of((n * per_chunk + g) * (8 * steps), 8 * steps)
            mixed = dot(lhs_ref[pl.ds(at, 8 * steps), :], here[g])
            to = pl.multiple_of((n * per_chunk + g) * 8, 8)
            for s in range(steps):
                z_ref[s, pl.ds(to, 8), :] = mixed[s * 8 : (s + 1) * 8]

    inv = inv_ref[...]
    results = [dot(inv, z_ref[s].astype(BF16)) for s in range(steps)]
    if packed:
        devices = out_ref.shape[0]
        results = [r.reshape(devices, span // devices, channels) for r in results]
        out_ref[...] = jnp.concatenate(results, axis=1).astype(BF16)
    else:
        for s in range(steps):
            out_ref[s] = results[s].astype(BF16)


def adjoint_kernel(
    extra, sec_ref, x_ref, lat_ref, inv_ref, all_ref, coeff_ref, out_ref, weights_ref,
    lhs_ref, z_ref, sems
):
    chunk = weight_copies(sec_ref, all_ref, weights_ref, sems)
    channels = x_ref.shape[-1]
    groups = lat_ref.shape[0] // 16
    if extra:
        wide = x_ref[...].astype(F32)
        size = wide.shape[1] - extra
        sums = jnp.sum(wide[:, size:], axis=0)
        x = wide[:, :size].reshape(-1, channels).astype(BF16)
    else:
        x = x_ref[...]
    value = dot(lat_ref[...], x).astype(BF16)
    coeff_ref[...] = value
    for n, part in enumerate(spread_pairs(value.astype(F32), 8, 1.0)):
        lhs_ref[:, n * channels : (n + 1) * channels] = part

    block = weights_ref.shape[0] // sems.shape[0]
    per_chunk = groups // sems.shape[0]

    @pl.loop(0, sems.shape[0])
    def _(n):
        chunk(n).wait()
        here = weights_ref[pl.ds(n * block, block)].reshape(per_chunk, 8, 2, channels, channels)
        for g in range(per_chunk):
            at = pl.multiple_of((n * per_chunk + g) * 16, 16)
            mixed = jnp.zeros((16, channels), F32)
            for t in range(8):
                left = lhs_ref[pl.ds(at, 16), 2 * t * channels : (2 * t + 2) * channels]
                right = jnp.concatenate([here[g, t, 0], here[g, t, 1]], axis=1)
                mixed = mixed + dot(left, right, ((1,), (1,)))
            z_ref[pl.ds(at, 16), :] = mixed

    result = dot(inv_ref[...], z_ref[...].astype(BF16))
    if extra:
        count = out_ref.shape[0]
        result = result.reshape(count, -1, channels)
        sums = jnp.broadcast_to(sums[None], (count, extra, channels))
        result = jnp.concatenate([result, sums], axis=1)
    out_ref[...] = result.astype(BF16)


def slope_kernel(
    step, rows, packed, sec_ref, recv_ref, state_ref, synth_ref, mix_ref, bias_ref, out_ref
):
    channels = mix_ref.shape[0]
    cells = state_ref.shape[2]
    modes = unpack_rows(recv_ref[...], range(step * rows, (step + 1) * rows), packed)
    mixing = mix_ref[...]
    bias = bias_ref[...]
    tile = 256
    for w in range(0, cells, tile):
        smooth = dot(synth_ref[w : w + tile, :], modes)
        for r in range(rows):
            linear = dot(state_ref[0, r, w : w + tile, :], mixing)
            pre = smooth[:, r * channels : (r + 1) * channels] + linear + bias
            out_ref[r, w : w + tile, :] = gelu_derivative(pre)


def finish_tile(
    r, w, tile, carried, slope_ref, state_ref, low_ref
):
    low = (carried.astype(F32) * slope_ref[r, w : w + tile, :]).astype(BF16)
    low_ref[r, w : w + tile, :] = low
    term = dot(state_ref[0, r, w : w + tile, :], low, ((0,), (0,)))
    return low, term


def start_kernel(
    packed, devices, sec_ref, cot_ref, slope_ref, state_ref, synth_ref, low_ref, send_ref, acc_ref
):
    rows, cells, channels = cot_ref.shape
    tile = 256
    spec, acc = None, None
    for w in range(0, cells, tile):
        lows = []
        for r in range(rows):
            low, term = finish_tile(
                r, w, tile, cot_ref[r, w : w + tile, :], slope_ref, state_ref, low_ref
            )
            lows.append(low)
            acc = term if acc is None else acc + term
        part = dot(synth_ref[:, w : w + tile], jnp.concatenate(lows, axis=1))
        spec = part if spec is None else spec + part
    acc_ref[...] = acc
    send_ref[...] = pack_rows(spec, rows, packed, devices)


def gradient_tile(r, w, tile, spread, carried_ref, low_ref, mixing):
    channels = mixing.shape[0]
    linear = dot(low_ref[r, w : w + tile, :], mixing, ((1,), (1,)))
    total = (
        carried_ref[r, w : w + tile, :].astype(F32)
        + linear
        + spread[:, r * channels : (r + 1) * channels]
    )
    return total.astype(BF16)


def turn_kernel(
    packed,
    devices,
    row_devs,
    last,
    sec_ref,
    recv_ref,
    carried_ref,
    prev_ref,
    slope_ref,
    state_ref,
    basis_ref,
    synth_ref,
    mix_ref,
    acc_in_ref,
    grad_ref,
    low_ref,
    send_ref,
    acc_ref,
):
    rows, cells, channels = prev_ref.shape
    carried_ref = carried_ref.at[0]
    here = grad_ref.at[1 if last else 0]
    modes = unpack_rows(recv_ref[...], range(rows), packed)
    mixing = mix_ref[...]
    tile = 256
    spec, acc = None, acc_in_ref[...]
    for w in range(0, cells, tile):
        spread = dot(basis_ref[w : w + tile, :], modes)
        lows = []
        for r in range(rows):
            grad = gradient_tile(r, w, tile, spread, carried_ref, prev_ref, mixing)
            here[r, w : w + tile, :] = grad
            low, term = finish_tile(r, w, tile, grad, slope_ref, state_ref, low_ref)
            if last:
                base = grad.astype(F32) + dot(low, mixing, ((1,), (1,)))
                grad_ref[0, r, w : w + tile, :] = base.astype(BF16)
            lows.append(low)
            acc = acc + term
        part = dot(synth_ref[:, w : w + tile], jnp.concatenate(lows, axis=1))
        spec = part if spec is None else spec + part
    acc_ref[...] = acc
    if last and packed:
        parts = [
            spec[:, r * channels : (r + 1) * channels].reshape(devices, 8, channels)
            for r in range(rows)
        ]
        terms = acc.reshape(row_devs, channels // row_devs, channels)
        parts.append(jnp.concatenate([terms] * (devices // row_devs), axis=0))
        send_ref[...] = jnp.concatenate(parts, axis=1).astype(BF16)
    else:
        send_ref[...] = pack_rows(spec, rows, packed, devices)


def close_kernel(
    packed, sec_ref, *refs
):
    count = (len(refs) - 2) // 2
    piece_refs, mode_refs = refs[:count], refs[count : 2 * count]
    basis_ref, out_ref = refs[2 * count :]
    turn = pl.program_id(0)
    rows, cells, channels = out_ref.shape
    tile = 256

    for d in range(count):

        @pl.when((turn == d) & (sec_ref[0] != 0))
        def _():
            out_ref[...] = piece_refs[d][...]

        @pl.when((turn == d) & (sec_ref[0] == 0))
        def _():
            if packed:
                wides = [ref[...].astype(F32) for ref in mode_refs]
                modes = []
                for r in range(rows):
                    at = (d * rows + r) * 8
                    parts = [wide[:, at : at + 8].reshape(-1, channels) for wide in wides]
                    modes.append(jnp.concatenate(parts, axis=0))
                modes = jnp.concatenate(modes, axis=1).astype(BF16)
            else:
                modes = []
                for r in range(rows):
                    parts = [ref[d * rows + r].astype(F32) for ref in mode_refs]
                    modes.append(jnp.concatenate(parts, axis=0))
                modes = jnp.concatenate(modes, axis=1).astype(BF16)
            for w in range(0, cells, tile):
                spread = dot(basis_ref[w : w + tile, :], modes)
                for r in range(rows):
                    base = piece_refs[d][r, w : w + tile, :].astype(F32)
                    total = base + spread[:, r * channels : (r + 1) * channels]
                    out_ref[r, w : w + tile, :] = total.astype(BF16)


def weight_kernel(steps, sec_ref, early_ref, late_ref, out_ref):
    channels = out_ref.shape[-1]
    tall = early_ref.shape[2]
    groups = tall // 8
    lefts = [early_ref[0, s] for s in range(steps)]
    rights = [early_ref[0, steps + s] for s in range(steps - 1)] + [late_ref[0]]
    rights = [rights[-1]] + rights[:-1]

    def tallied(values):
        wide = [v.astype(F32).reshape(groups, 8, channels) for v in values]
        return jnp.concatenate(wide, axis=1).reshape(groups * steps * 8, channels)

    span = steps * 8
    left, right = tallied(lefts), tallied(rights)
    ids = lax.broadcasted_iota(jnp.int32, right.shape, 0)
    turned = jnp.where(
        ids % 2 == 0,
        pltpu.roll(right, groups * span - 1, 0),
        -pltpu.roll(right, 1, 0),
    )
    right = jnp.concatenate([right, turned], axis=1).astype(BF16)
    pair = (ids // 2) % 4
    lefts = [jnp.where(pair == t, left, 0.0).astype(BF16) for t in range(4)]
    per_j = out_ref.shape[1]
    for g in range(groups):
        rhs = right[g * span : (g + 1) * span]
        for t in range(4):
            product = dot(lefts[t][g * span : (g + 1) * span], rhs, ((0,), (0,))).astype(BF16)
            j, k = divmod(g * 4 + t, per_j)
            out_ref[j, k, 0] = product[:, :channels]
            out_ref[j, k, 1] = product[:, channels:]


def whole(shape):
    return pl.BlockSpec(shape, lambda *_: (0,) * len(shape))


def call(kernel, outs, in_specs, operands, grid=(1,), out_specs=None, scratch=(), prefetch=None,
         flops=0, moved=0, aliases=None):
    if out_specs is None:
        out_specs = [whole(o.shape) for o in outs]
    count = 0 if prefetch is None else 1
    lead = () if prefetch is None else (prefetch,)
    return pl.pallas_call(
        kernel,
        out_shape=outs,
        grid_spec=pltpu.PrefetchScalarGridSpec(
            num_scalar_prefetch=count,
            grid=grid,
            in_specs=in_specs,
            out_specs=out_specs,
            scratch_shapes=list(scratch),
        ),
        input_output_aliases=aliases or {},
        compiler_params=pltpu.CompilerParams(
            vmem_limit_bytes=VMEM_LIMIT, dimension_semantics=("arbitrary",) * len(grid)
        ),
        cost_estimate=pl.CostEstimate(flops=flops, bytes_accessed=moved, transcendentals=0),
    )(*lead, *operands)


def local(states, cotangent, spec_weights, local_weight, bias):
    sections = lax.axis_size("section")
    row_devs = lax.axis_size("row")
    section = lax.axis_index("section")
    devices = sections * row_devs
    channels = local_weight.shape[0]
    cells = states.shape[2]
    rows_here = states.shape[1]
    rows = rows_here // sections
    freqs = spec_weights.shape[0]
    row_modes = spec_weights.shape[1]
    modes = row_modes // sections
    parts = 2 * modes
    lat_cells = rows_here * row_devs
    packed = parts == 8
    sec = section.astype(jnp.int32).reshape(1)

    order = (
        np.arange(row_devs)[None, :, None] * row_modes
        + np.arange(sections)[:, None, None] * modes
        + np.arange(modes)[None, None, :]
    ).reshape(-1)
    basis_np, synth_np = lon_tables(order, cells)
    basis = jnp.asarray(basis_np, BF16)
    basis_t = jnp.asarray(basis_np.T, BF16)
    synth = jnp.asarray(synth_np, BF16)
    synth_t = jnp.asarray(synth_np.T, BF16)
    row_order = (
        np.arange(row_devs)[None, :, None] * rows_here
        + np.arange(sections)[:, None, None] * rows
        + np.arange(rows)[None, None, :]
    ).reshape(-1)
    lat_plain = jnp.asarray(lat_matrices(np.arange(lat_cells), freqs, lat_cells, modes), BF16)
    shared_np = lat_matrices(row_order, freqs, lat_cells, modes)
    lat_shared = jnp.asarray(shared_np, BF16)
    inv_shared = jnp.asarray(shared_np.T, BF16)
    inv_plain = jnp.asarray(lat_matrices(np.arange(lat_cells), freqs, lat_cells, modes).T, BF16)
    mode_rows = lat_plain.shape[0]
    grid_rows = lat_plain.shape[1]

    def exchange(values):
        return lax.all_to_all(values, ALL, 0, 0, tiled=True)

    def share(piece, d):
        return lax.ppermute(piece, "section", [(i, i ^ d) for i in range(sections)])

    own = states[0].reshape(sections, rows, cells, channels)
    pieces = [lax.dynamic_index_in_dim(own, section, 0, False)]
    for d in range(1, sections):
        pieces.append(share(lax.dynamic_index_in_dim(own, section ^ d, 0, False), d))

    total = basis_t.shape[0]
    out_shape = (devices, rows_here * 8, channels) if packed else (rows_here, total, channels)
    (spectra,) = call(
        functools.partial(spectra_kernel, 2, packed, devices),
        [jax.ShapeDtypeStruct(out_shape, BF16)],
        [whole(states.shape[1:]), whole(basis_t.shape)],
        (states[0], basis_t),
        flops=2 * total * cells * rows_here * channels,
        moved=4 * rows_here * cells * channels,
    )
    if not packed:
        spectra = outer_pack(spectra, devices)
    gathered = exchange(spectra)
    gathered, *pieces = lax.optimization_barrier((gathered, *pieces))
    gathered = gathered.reshape(sections * grid_rows, channels)
    all_states = jnp.stack(pieces, 0)

    chunk_j = max(1, min(freqs, CHUNK // modes))
    weight_scratch = [pltpu.VMEM((freqs, modes, 2, channels, channels), BF16)]
    weight_sems = [pltpu.SemaphoreType.DMA((freqs // chunk_j,))]
    weight_spec = pl.BlockSpec(memory_space=pl.ANY)
    weight_bytes = 4 * freqs * modes * channels * channels
    mixed_shape = (
        (devices, sections * rows * parts, channels)
        if packed
        else (sections, grid_rows, channels)
    )
    coeffs, mixed = call(
        functools.partial(mix_kernel, sections, packed),
        [
            jax.ShapeDtypeStruct((sections, mode_rows, channels), BF16),
            jax.ShapeDtypeStruct(mixed_shape, BF16),
        ],
        [whole(gathered.shape), whole(lat_plain.shape), whole(inv_shared.shape), weight_spec],
        (gathered, lat_plain, inv_shared, spec_weights),
        scratch=weight_scratch
        + [
            pltpu.VMEM((sections * mode_rows, 8 * channels), BF16),
            pltpu.VMEM((sections, mode_rows, channels), F32),
        ]
        + weight_sems,
        prefetch=sec,
        flops=4 * weight_bytes,
        moved=weight_bytes,
    )
    if not packed:
        mixed = mixed.reshape(sections, devices, rows * parts, channels).transpose(1, 0, 2, 3)
        mixed = mixed.reshape(devices, sections * rows * parts, channels)
    back = exchange(mixed)
    if not packed:
        back = outer_unpack(back, sections * rows)

    field_block = (1, rows, cells, channels)
    shape3 = (rows, cells, channels)
    bias2 = bias.reshape(1, channels)
    slopes = [None] * sections
    for s in range(sections - 1, -1, -1):
        (slopes[s],) = call(
            functools.partial(slope_kernel, s, rows, packed),
            [jax.ShapeDtypeStruct(shape3, F32)],
            [
                whole(back.shape),
                pl.BlockSpec(field_block, functools.partial(lambda s, b, i: (i[0] ^ s, 0, 0, 0), s)),
                whole(synth_t.shape),
                whole(local_weight.shape),
                whole(bias2.shape),
            ],
            (back, all_states, synth_t, local_weight, bias2),
            prefetch=sec,
            flops=2 * total * cells * rows * channels,
            moved=10 * rows * cells * channels,
        )

    send_shape = (devices, rows * 8, channels) if packed else (rows, total, channels)
    turn_outs = [
        jax.ShapeDtypeStruct(shape3, BF16),
        jax.ShapeDtypeStruct(send_shape, BF16),
        jax.ShapeDtypeStruct((channels, channels), F32),
    ]

    def state_spec(s):
        return pl.BlockSpec(field_block, lambda b, i: (i[0] ^ s, 0, 0, 0))

    s = sections - 1
    carried = lax.dynamic_slice_in_dim(cotangent, section * rows, rows, 0)
    low, send, acc = call(
        functools.partial(start_kernel, packed, devices),
        turn_outs,
        [whole(shape3), whole(shape3), state_spec(s), whole(synth.shape)],
        (carried, slopes[s], all_states, synth),
        prefetch=sec,
        flops=2 * total * cells * rows * channels,
        moved=10 * rows * cells * channels,
    )
    cots = [None] * sections
    slot = channels // row_devs
    store = carried[None]
    store_shape = (sections,) + shape3
    for s in range(sections - 1, -1, -1):
        extra = 0
        if s == 0:
            extra = slot
            if not packed:
                terms = acc.reshape(row_devs, slot, channels).astype(BF16)
                terms = jnp.concatenate([terms] * sections, axis=0)
                send = jnp.concatenate([outer_pack(send, devices), terms], axis=1)
        elif not packed:
            send = outer_pack(send, devices)
        got = exchange(send)
        if extra and not packed:
            sums = jnp.sum(got[:, rows * parts :].astype(F32), 0)
            got = got[:, : rows * parts]
        inside = extra if packed else 0
        if not inside:
            got = got.reshape(grid_rows, channels)
        inner_shape = (grid_rows, channels)
        if inside:
            inner_shape = (row_devs, grid_rows // row_devs + extra, channels)
        inverse = inv_shared if s > 0 else inv_plain
        cots[s], inner = call(
            functools.partial(adjoint_kernel, inside),
            [
                jax.ShapeDtypeStruct((mode_rows, channels), BF16),
                jax.ShapeDtypeStruct(inner_shape, BF16),
            ],
            [whole(got.shape), whole(lat_shared.shape), whole(inverse.shape), weight_spec],
            (got, lat_shared, inverse, spec_weights),
            scratch=weight_scratch
            + [
                pltpu.VMEM((mode_rows, 16 * channels), BF16),
                pltpu.VMEM((mode_rows, channels), F32),
            ]
            + weight_sems,
            prefetch=sec,
            flops=2 * weight_bytes,
            moved=weight_bytes,
        )
        if s == 0:
            break
        got = exchange(inner.reshape(devices, rows * parts, channels))
        if not packed:
            got = outer_unpack(got, rows)
        last = s == 1
        first = s == sections - 1
        if last and packed:
            turn_outs[1] = jax.ShapeDtypeStruct((devices, rows * 8 + slot, channels), BF16)
        carried_at = 0 if first else s + 1
        span = 2 if last else 1
        grad_at = 0 if last else s
        store, low, send, acc = call(
            functools.partial(turn_kernel, packed, devices, row_devs, last),
            [jax.ShapeDtypeStruct(store_shape, BF16)] + turn_outs,
            [
                whole(got.shape),
                pl.BlockSpec(field_block, functools.partial(lambda n, *_: (n, 0, 0, 0), carried_at)),
                whole(shape3),
                whole(shape3),
                state_spec(s - 1),
                whole(basis.shape),
                whole(synth.shape),
                whole(local_weight.shape),
                whole(acc.shape),
            ],
            (got, store, low, slopes[s - 1], all_states, basis, synth, local_weight, acc),
            out_specs=[
                pl.BlockSpec(
                    (span,) + shape3, functools.partial(lambda n, *_: (n, 0, 0, 0), grad_at)
                )
            ]
            + [whole(o.shape) for o in turn_outs],
            prefetch=sec,
            aliases={} if first else {2: 0},
            flops=4 * total * cells * rows * channels,
            moved=16 * rows * cells * channels,
        )

    parts_of = [lax.dynamic_index_in_dim(store, section, 0, False)]
    for d in range(1, sections):
        parts_of.append(share(lax.dynamic_index_in_dim(store, section ^ d, 0, False), d))

    part = mode_rows // sections

    def gather_modes(values):
        mine = [lax.dynamic_index_in_dim(values, section ^ d, 0, False) for d in range(sections)]
        return jnp.stack([mine[0]] + [share(mine[d], d) for d in range(1, sections)], 0)

    early = jnp.concatenate([coeffs, jnp.stack(cots[1:], 0)], 0)
    early = early.reshape(-1, sections, part, channels).swapaxes(0, 1)
    early = gather_modes(early)

    if not packed:
        inner = inner.reshape(row_devs, grid_rows // row_devs, channels)
        both = jnp.broadcast_to(sums.astype(BF16)[None], (row_devs, slot, channels))
        inner = jnp.concatenate([inner, both], axis=1)
    got = lax.all_to_all(inner, "row", 0, 0, tiled=True)
    size = grid_rows // row_devs
    local_total = got[:, size:].reshape(channels, channels).astype(F32)
    d_local = local_total * lax.rsqrt(jnp.float32(sections * lat_cells * cells))
    if not packed:
        got = outer_unpack(got[:, :size], rows_here)
    mode_parts = [got] + [
        lax.ppermute(got, "section", [(d, 0)]) for d in range(1, sections)
    ]

    late = gather_modes(cots[0].reshape(sections, part, channels))
    own_freqs = freqs // sections
    own_j = max(1, min(own_freqs, 32 // modes))
    tall = own_j * parts
    (d_spectral,) = call(
        functools.partial(weight_kernel, sections),
        [jax.ShapeDtypeStruct((own_freqs, row_modes, 2, channels, channels), BF16)],
        [
            pl.BlockSpec((1, 2 * sections - 1, tall, channels), lambda a, b, i: (a, 0, b, 0)),
            pl.BlockSpec((1, tall, channels), lambda a, b, i: (a, b, 0)),
        ],
        (early, late),
        grid=(sections, own_freqs // own_j),
        out_specs=[
            pl.BlockSpec(
                (own_j, modes, 2, channels, channels), lambda a, b, i: (b, i[0] ^ a, 0, 0, 0)
            )
        ],
        prefetch=sec,
        flops=8 * weight_bytes,
        moved=weight_bytes,
    )

    (grad_states,) = call(
        functools.partial(close_kernel, packed),
        [jax.ShapeDtypeStruct((rows_here, cells, channels), BF16)],
        [whole(shape3)] * sections + [whole(got.shape)] * sections + [whole(basis.shape)],
        (*parts_of, *mode_parts, basis),
        grid=(sections,),
        out_specs=[pl.BlockSpec(shape3, lambda d, i: (i[0] ^ d, 0, 0))],
        prefetch=sec,
        flops=2 * total * cells * rows_here * channels,
        moved=8 * rows_here * cells * channels,
    )
    return (grad_states[None], d_spectral, d_local)


def solution(mesh):
    return jax.shard_map(
        local,
        mesh=mesh,
        in_specs=(
            P("section", "row", None, None),
            P("row", None, None),
            P(None, "row", None, None, None),
            P(),
            P(),
        ),
        out_specs=(P("section", "row", None, None), P("section", "row", None, None, None), P()),
        check_vma=False,
    )
```

```python
import functools
import math

import jax
import jax.numpy as jnp
import numpy as np
from jax import lax
from jax.experimental import pallas as pl
from jax.experimental.pallas import tpu as pltpu
from jax.sharding import PartitionSpec as P

GELU_SLOPE = math.sqrt(2.0 / math.pi)
GELU_CUBIC = 0.044715
BF16 = jnp.bfloat16
F32 = jnp.float32
ALL = ("section", "row")
VMEM_LIMIT = 56 * 1024 * 1024
CHUNK = 32


def gelu_derivative(values):
    square = values * values
    inner_arg = GELU_SLOPE * values * (1.0 + GELU_CUBIC * square)
    tangent = jnp.tanh(inner_arg)
    return 0.5 * (1.0 + tangent) + (0.5 * GELU_SLOPE) * values * (1.0 - tangent * tangent) * (
        1.0 + 3.0 * GELU_CUBIC * square
    )


def lon_tables(mode_list, lon_cells):
    phases = np.arange(lon_cells)[:, None] * mode_list[None, :] % lon_cells
    angles = phases * (2.0 * math.pi / lon_cells)
    factor = 1.0 / math.sqrt(lon_cells)
    forward = np.stack([np.cos(angles), -np.sin(angles)], 2) * factor
    doubling = np.where(mode_list == 0, 1.0, 2.0)
    backward = np.transpose(forward, (1, 2, 0)) * doubling[:, None, None]
    return (
        forward.reshape(lon_cells, -1).astype(np.float32),
        backward.reshape(-1, lon_cells).astype(np.float32),
    )


def lat_matrices(row_list, freq_count, lat_cells, modes):
    freq = np.arange(freq_count)
    signed = np.where(freq < freq_count // 2, freq, freq - freq_count)
    angles = ((signed % lat_cells)[:, None] * row_list[None, :] % lat_cells) * (
        2.0 * math.pi / lat_cells
    )
    factor = 1.0 / math.sqrt(lat_cells)
    cos, sin = np.cos(angles) * factor, np.sin(angles) * factor
    same = np.eye(modes)
    rot = np.array([[[1.0, 0.0], [0.0, 1.0]], [[0.0, 1.0], [-1.0, 0.0]]])
    block = cos[:, None, None, :, None, None] * same[None, :, None, None, :, None] * rot[0][
        None, None, :, None, None, :
    ] + sin[:, None, None, :, None, None] * same[None, :, None, None, :, None] * rot[1][
        None, None, :, None, None, :
    ]
    return block.reshape(freq_count * modes * 2, row_list.size * modes * 2).astype(np.float32)


def dot(a, b, contract=((1,), (0,))):
    return lax.dot_general(a, b, (contract, ((), ())), preferred_element_type=F32)


def unpack_rows(values, rows, packed):
    channels = values.shape[-1]
    if packed:
        devices, per_dev, _ = values.shape
        wide = values.astype(F32).reshape(devices, per_dev // 8, 8, channels)
        parts = [wide[:, r].reshape(devices * 8, channels) for r in rows]
    else:
        parts = [values[r].astype(F32) for r in rows]
    return jnp.concatenate(parts, axis=1).astype(BF16)


def pack_rows(spec, row_count, packed, devices):
    channels = spec.shape[1] // row_count
    parts = [spec[:, r * channels : (r + 1) * channels] for r in range(row_count)]
    if packed:
        parts = [p.reshape(devices, 8, channels) for p in parts]
        return jnp.concatenate(parts, axis=1).astype(BF16)
    return jnp.stack(parts, 0).astype(BF16)


def outer_pack(spec, devices):
    rows, total, channels = spec.shape
    per = total // devices
    return spec.reshape(rows, devices, per, channels).transpose(1, 0, 2, 3).reshape(
        devices, rows * per, channels
    )


def outer_unpack(received, row_count):
    devices, total, channels = received.shape
    per = total // row_count
    return received.reshape(devices, row_count, per, channels).transpose(1, 0, 2, 3).reshape(
        row_count, devices * per, channels
    )


def spectra_kernel(rows_at_once, packed, devices, fields_ref, basis_ref, out_ref):
    basis = basis_ref[...]
    row_count = fields_ref.shape[0]
    for first in range(0, row_count, rows_at_once):
        field = jnp.concatenate([fields_ref[first + r] for r in range(rows_at_once)], axis=1)
        spec = pack_rows(dot(basis, field), rows_at_once, packed, devices)
        if packed:
            out_ref[:, first * 8 : (first + rows_at_once) * 8, :] = spec
        else:
            out_ref[first : first + rows_at_once] = spec


def spread_pairs(values, per_group, sign):
    rows, _ = values.shape
    ids = lax.broadcasted_iota(jnp.int32, values.shape, 0)
    after = pltpu.roll(values, rows - 1, 0)
    before = pltpu.roll(values, 1, 0)
    turned = jnp.where(ids % 2 == 0, sign * after, -sign * before)
    pair = (ids // 2) % per_group
    parts = []
    for t in range(per_group):
        parts.append(jnp.where(pair == t, values, 0.0).astype(BF16))
        parts.append(jnp.where(pair == t, turned, 0.0).astype(BF16))
    return parts


def start_copies(sec_ref, all_ref, weights_ref, sems, early, late=()):
    chunks = sems.shape[0] - len(early) - len(late)
    span = weights_ref.shape[0] // chunks
    modes = weights_ref.shape[1]
    first = sec_ref[0] * modes

    def chunk(n):
        return pltpu.make_async_copy(
            all_ref.at[pl.ds(n * span, span), pl.ds(first, modes)],
            weights_ref.at[pl.ds(n * span, span)],
            sems.at[n],
        )

    small = [
        pltpu.make_async_copy(source, target, sems.at[chunks + n])
        for n, (source, target) in enumerate((*early, *late))
    ]
    for copy in small[: len(early)]:
        copy.start()
    for n in range(chunks):
        chunk(n).start()
    for copy in small[len(early) :]:
        copy.start()
    return chunk, chunks, small


def mix_kernel(
    steps, packed, sec_ref, x_any, lat_any, inv_any, all_ref, coeff_ref, out_ref, weights_ref,
    x_ref, lat_ref, inv_ref, lhs_ref, z_ref, sems
):
    chunk, chunks, small = start_copies(
        sec_ref, all_ref, weights_ref, sems, [(x_any, x_ref), (lat_any, lat_ref)],
        [(inv_any, inv_ref)],
    )
    small[0].wait()
    small[1].wait()
    channels = x_ref.shape[-1]
    span = x_ref.shape[0] // steps
    groups = lat_ref.shape[0] // 8
    lat = lat_ref[...]
    found = []
    for s in range(steps):
        value = dot(lat, x_ref[s * span : (s + 1) * span, :]).astype(BF16)
        coeff_ref[s] = value
        found.append(value.astype(F32).reshape(groups, 8, channels))
    tall = jnp.concatenate(found, axis=1).reshape(groups * steps * 8, channels)
    for n, part in enumerate(spread_pairs(tall, 4, -1.0)):
        lhs_ref[:, n * channels : (n + 1) * channels] = part

    block = weights_ref.shape[0] // chunks
    per_chunk = groups // chunks

    @pl.loop(0, chunks)
    def _(n):
        chunk(n).wait()
        here = weights_ref[pl.ds(n * block, block)].reshape(per_chunk, 8 * channels, channels)
        for g in range(per_chunk):
            at = pl.multiple_of((n * per_chunk + g) * (8 * steps), 8 * steps)
            mixed = dot(lhs_ref[pl.ds(at, 8 * steps), :], here[g])
            to = pl.multiple_of((n * per_chunk + g) * 8, 8)
            for s in range(steps):
                z_ref[s, pl.ds(to, 8), :] = mixed[s * 8 : (s + 1) * 8]

    small[2].wait()
    inv = inv_ref[...]
    results = [dot(inv, z_ref[s].astype(BF16)) for s in range(steps)]
    if packed:
        devices = out_ref.shape[0]
        results = [r.reshape(devices, span // devices, channels) for r in results]
        out_ref[...] = jnp.concatenate(results, axis=1).astype(BF16)
    else:
        for s in range(steps):
            out_ref[s] = results[s].astype(BF16)


def adjoint_kernel(
    extra, sec_ref, x_any, lat_any, inv_any, all_ref, coeff_ref, out_ref, weights_ref, x_ref,
    lat_ref, inv_ref, lhs_ref, z_ref, sems
):
    copies = start_copies(
        sec_ref, all_ref, weights_ref, sems, [(x_any, x_ref), (lat_any, lat_ref)],
        [(inv_any, inv_ref)],
    )
    copies[2][0].wait()
    copies[2][1].wait()
    channels = x_ref.shape[-1]
    if extra:
        wide = x_ref[...].astype(F32)
        size = wide.shape[1] - extra
        sums = jnp.sum(wide[:, size:], axis=0)
        x = wide[:, :size].reshape(-1, channels).astype(BF16)
    else:
        x = x_ref[...]
    value = dot(lat_ref[...], x).astype(BF16)
    coeff_ref[...] = value
    result = adjoint_mix(value, copies, weights_ref, inv_ref, lhs_ref, z_ref)
    if extra:
        count = out_ref.shape[0]
        result = result.reshape(count, -1, channels)
        sums = jnp.broadcast_to(sums[None], (count, extra, channels))
        result = jnp.concatenate([result, sums], axis=1)
    out_ref[...] = result.astype(BF16)


def adjoint_mix(value, copies, weights_ref, inv_ref, lhs_ref, z_ref):
    chunk, chunks, small = copies
    channels = value.shape[-1]
    groups = value.shape[0] // 16
    for n, part in enumerate(spread_pairs(value.astype(F32), 8, 1.0)):
        lhs_ref[:, n * channels : (n + 1) * channels] = part

    block = weights_ref.shape[0] // chunks
    per_chunk = groups // chunks

    @pl.loop(0, chunks)
    def _(n):
        chunk(n).wait()
        here = weights_ref[pl.ds(n * block, block)].reshape(per_chunk, 8, 2, channels, channels)
        for g in range(per_chunk):
            at = pl.multiple_of((n * per_chunk + g) * 16, 16)
            mixed = jnp.zeros((16, channels), F32)
            for t in range(8):
                left = lhs_ref[pl.ds(at, 16), 2 * t * channels : (2 * t + 2) * channels]
                right = jnp.concatenate([here[g, t, 0], here[g, t, 1]], axis=1)
                mixed = mixed + dot(left, right, ((1,), (1,)))
            z_ref[pl.ds(at, 16), :] = mixed

    small[-1].wait()
    return dot(inv_ref[...], z_ref[...].astype(BF16))


def slope_kernel(
    step, rows, packed, sec_ref, recv_ref, state_ref, synth_ref, mix_ref, bias_ref, out_ref
):
    channels = mix_ref.shape[0]
    cells = state_ref.shape[2]
    modes = unpack_rows(recv_ref[...], range(step * rows, (step + 1) * rows), packed)
    mixing = mix_ref[...]
    bias = bias_ref[...]
    tile = 256
    for w in range(0, cells, tile):
        smooth = dot(synth_ref[w : w + tile, :], modes)
        for r in range(rows):
            linear = dot(state_ref[0, r, w : w + tile, :], mixing)
            pre = smooth[:, r * channels : (r + 1) * channels] + linear + bias
            out_ref[r, w : w + tile, :] = gelu_derivative(pre)


def finish_tile(
    r, w, tile, carried, slope_ref, state_ref, low_ref
):
    low = (carried.astype(F32) * slope_ref[r, w : w + tile, :]).astype(BF16)
    low_ref[r, w : w + tile, :] = low
    term = dot(state_ref[0, r, w : w + tile, :], low, ((0,), (0,)))
    return low, term


def start_kernel(
    packed, devices, sec_ref, cot_ref, slope_ref, state_ref, synth_ref, low_ref, send_ref, acc_ref
):
    rows, cells, channels = cot_ref.shape
    tile = 256
    spec, acc = None, None
    for w in range(0, cells, tile):
        lows = []
        for r in range(rows):
            low, term = finish_tile(
                r, w, tile, cot_ref[r, w : w + tile, :], slope_ref, state_ref, low_ref
            )
            lows.append(low)
            acc = term if acc is None else acc + term
        part = dot(synth_ref[:, w : w + tile], jnp.concatenate(lows, axis=1))
        spec = part if spec is None else spec + part
    acc_ref[...] = acc
    send_ref[...] = pack_rows(spec, rows, packed, devices)


def gradient_tile(r, w, tile, spread, carried_ref, low_ref, mixing):
    channels = mixing.shape[0]
    linear = dot(low_ref[r, w : w + tile, :], mixing, ((1,), (1,)))
    total = (
        carried_ref[r, w : w + tile, :].astype(F32)
        + linear
        + spread[:, r * channels : (r + 1) * channels]
    )
    return total.astype(BF16)


def turn_kernel(
    packed,
    devices,
    row_devs,
    last,
    sec_ref,
    recv_ref,
    carried_ref,
    prev_ref,
    slope_ref,
    state_ref,
    basis_ref,
    synth_ref,
    mix_ref,
    acc_in_ref,
    grad_ref,
    low_ref,
    send_ref,
    acc_ref,
):
    rows, cells, channels = prev_ref.shape
    carried_ref = carried_ref.at[0]
    here = grad_ref.at[1 if last else 0]
    modes = unpack_rows(recv_ref[...], range(rows), packed)
    mixing = mix_ref[...]
    tile = 256
    spec, acc = None, acc_in_ref[...]
    for w in range(0, cells, tile):
        spread = dot(basis_ref[w : w + tile, :], modes)
        lows = []
        for r in range(rows):
            grad = gradient_tile(r, w, tile, spread, carried_ref, prev_ref, mixing)
            here[r, w : w + tile, :] = grad
            low, term = finish_tile(r, w, tile, grad, slope_ref, state_ref, low_ref)
            if last:
                base = grad.astype(F32) + dot(low, mixing, ((1,), (1,)))
                grad_ref[0, r, w : w + tile, :] = base.astype(BF16)
            lows.append(low)
            acc = acc + term
        part = dot(synth_ref[:, w : w + tile], jnp.concatenate(lows, axis=1))
        spec = part if spec is None else spec + part
    acc_ref[...] = acc
    if last and packed:
        parts = [
            spec[:, r * channels : (r + 1) * channels].reshape(devices, 8, channels)
            for r in range(rows)
        ]
        terms = acc.reshape(row_devs, channels // row_devs, channels)
        parts.append(jnp.concatenate([terms] * (devices // row_devs), axis=0))
        send_ref[...] = jnp.concatenate(parts, axis=1).astype(BF16)
    else:
        send_ref[...] = pack_rows(spec, rows, packed, devices)


def close_kernel(
    packed, sec_ref, *refs
):
    count = (len(refs) - 2) // 2
    piece_refs, mode_refs = refs[:count], refs[count : 2 * count]
    basis_ref, out_ref = refs[2 * count :]
    turn = pl.program_id(0)
    rows, cells, channels = out_ref.shape
    tile = 256

    for d in range(count):

        @pl.when((turn == d) & (sec_ref[0] != 0))
        def _():
            out_ref[...] = piece_refs[d][...]

        @pl.when((turn == d) & (sec_ref[0] == 0))
        def _():
            if packed:
                wides = [ref[...].astype(F32) for ref in mode_refs]
                modes = []
                for r in range(rows):
                    at = (d * rows + r) * 8
                    parts = [wide[:, at : at + 8].reshape(-1, channels) for wide in wides]
                    modes.append(jnp.concatenate(parts, axis=0))
                modes = jnp.concatenate(modes, axis=1).astype(BF16)
            else:
                modes = []
                for r in range(rows):
                    parts = [ref[d * rows + r].astype(F32) for ref in mode_refs]
                    modes.append(jnp.concatenate(parts, axis=0))
                modes = jnp.concatenate(modes, axis=1).astype(BF16)
            for w in range(0, cells, tile):
                spread = dot(basis_ref[w : w + tile, :], modes)
                for r in range(rows):
                    base = piece_refs[d][r, w : w + tile, :].astype(F32)
                    total = base + spread[:, r * channels : (r + 1) * channels]
                    out_ref[r, w : w + tile, :] = total.astype(BF16)


def weight_kernel(steps, sec_ref, first_ref, late_ref, out_ref):
    channels = out_ref.shape[-1]
    tall = late_ref.shape[2]
    groups = tall // 8
    lefts = [first_ref[0, s] for s in range(steps)]
    rights = [late_ref[0, s] for s in range(steps - 1)] + [first_ref[0, steps]]

    def tallied(values):
        wide = [v.astype(F32).reshape(groups, 8, channels) for v in values]
        return jnp.concatenate(wide, axis=1).reshape(groups * steps * 8, channels)

    span = steps * 8
    left, right = tallied(lefts), tallied(rights)
    ids = lax.broadcasted_iota(jnp.int32, right.shape, 0)
    turned = jnp.where(
        ids % 2 == 0,
        pltpu.roll(right, groups * span - 1, 0),
        -pltpu.roll(right, 1, 0),
    )
    right = jnp.concatenate([right, turned], axis=1).astype(BF16)
    pair = (ids // 2) % 4
    lefts = [jnp.where(pair == t, left, 0.0).astype(BF16) for t in range(4)]
    per_j = out_ref.shape[1]
    for g in range(groups):
        rhs = right[g * span : (g + 1) * span]
        for t in range(4):
            product = dot(lefts[t][g * span : (g + 1) * span], rhs, ((0,), (0,))).astype(BF16)
            j, k = divmod(g * 4 + t, per_j)
            out_ref[j, k, 0] = product[:, :channels]
            out_ref[j, k, 1] = product[:, channels:]


def whole(shape):
    return pl.BlockSpec(shape, lambda *_: (0,) * len(shape))


def call(kernel, outs, in_specs, operands, grid=(1,), out_specs=None, scratch=(), prefetch=None,
         flops=0, moved=0, aliases=None):
    if out_specs is None:
        out_specs = [whole(o.shape) for o in outs]
    count = 0 if prefetch is None else 1
    lead = () if prefetch is None else (prefetch,)
    return pl.pallas_call(
        kernel,
        out_shape=outs,
        grid_spec=pltpu.PrefetchScalarGridSpec(
            num_scalar_prefetch=count,
            grid=grid,
            in_specs=in_specs,
            out_specs=out_specs,
            scratch_shapes=list(scratch),
        ),
        input_output_aliases=aliases or {},
        compiler_params=pltpu.CompilerParams(
            vmem_limit_bytes=VMEM_LIMIT, dimension_semantics=("arbitrary",) * len(grid)
        ),
        cost_estimate=pl.CostEstimate(flops=flops, bytes_accessed=moved, transcendentals=0),
    )(*lead, *operands)


def local(states, cotangent, spec_weights, local_weight, bias):
    sections = lax.axis_size("section")
    row_devs = lax.axis_size("row")
    section = lax.axis_index("section")
    devices = sections * row_devs
    channels = local_weight.shape[0]
    cells = states.shape[2]
    rows_here = states.shape[1]
    rows = rows_here // sections
    freqs = spec_weights.shape[0]
    row_modes = spec_weights.shape[1]
    modes = row_modes // sections
    parts = 2 * modes
    lat_cells = rows_here * row_devs
    packed = parts == 8
    sec = section.astype(jnp.int32).reshape(1)

    order = (
        np.arange(row_devs)[None, :, None] * row_modes
        + np.arange(sections)[:, None, None] * modes
        + np.arange(modes)[None, None, :]
    ).reshape(-1)
    basis_np, synth_np = lon_tables(order, cells)
    basis = jnp.asarray(basis_np, BF16)
    basis_t = jnp.asarray(basis_np.T, BF16)
    synth = jnp.asarray(synth_np, BF16)
    synth_t = jnp.asarray(synth_np.T, BF16)
    row_order = (
        np.arange(row_devs)[None, :, None] * rows_here
        + np.arange(sections)[:, None, None] * rows
        + np.arange(rows)[None, None, :]
    ).reshape(-1)
    lat_plain = jnp.asarray(lat_matrices(np.arange(lat_cells), freqs, lat_cells, modes), BF16)
    shared_np = lat_matrices(row_order, freqs, lat_cells, modes)
    lat_shared = jnp.asarray(shared_np, BF16)
    inv_shared = jnp.asarray(shared_np.T, BF16)
    inv_plain = jnp.asarray(lat_matrices(np.arange(lat_cells), freqs, lat_cells, modes).T, BF16)
    mode_rows = lat_plain.shape[0]
    grid_rows = lat_plain.shape[1]

    def exchange(values):
        return lax.all_to_all(values, ALL, 0, 0, tiled=True)

    def share(piece, d):
        return lax.ppermute(piece, "section", [(i, i ^ d) for i in range(sections)])

    own = states[0].reshape(sections, rows, cells, channels)
    pieces = [lax.dynamic_index_in_dim(own, section, 0, False)]
    for d in range(1, sections):
        pieces.append(share(lax.dynamic_index_in_dim(own, section ^ d, 0, False), d))

    total = basis_t.shape[0]
    out_shape = (devices, rows_here * 8, channels) if packed else (rows_here, total, channels)
    (spectra,) = call(
        functools.partial(spectra_kernel, 2, packed, devices),
        [jax.ShapeDtypeStruct(out_shape, BF16)],
        [whole(states.shape[1:]), whole(basis_t.shape)],
        (states[0], basis_t),
        flops=2 * total * cells * rows_here * channels,
        moved=4 * rows_here * cells * channels,
    )
    if not packed:
        spectra = outer_pack(spectra, devices)
    gathered = exchange(spectra)
    near = sections - 1
    gathered, *pieces[:near] = lax.optimization_barrier((gathered, *pieces[:near]))
    gathered = gathered.reshape(sections * grid_rows, channels)
    all_states = jnp.stack(pieces[:near] + [jnp.zeros_like(pieces[0])], 0)
    all_states = lax.optimization_barrier(all_states)
    all_states = lax.dynamic_update_slice_in_dim(all_states, pieces[near][None], near, 0)

    chunk_j = max(1, min(freqs, CHUNK // modes))
    weight_scratch = [pltpu.VMEM((freqs, modes, 2, channels, channels), BF16)]
    chunks = freqs // chunk_j
    anywhere = pl.BlockSpec(memory_space=pl.ANY)
    weight_bytes = 4 * freqs * modes * channels * channels
    mixed_shape = (
        (devices, sections * rows * parts, channels)
        if packed
        else (sections, grid_rows, channels)
    )
    coeffs, mixed = call(
        functools.partial(mix_kernel, sections, packed),
        [
            jax.ShapeDtypeStruct((sections, mode_rows, channels), BF16),
            jax.ShapeDtypeStruct(mixed_shape, BF16),
        ],
        [anywhere] * 4,
        (gathered, lat_plain, inv_shared, spec_weights),
        scratch=weight_scratch
        + [
            pltpu.VMEM(gathered.shape, BF16),
            pltpu.VMEM(lat_plain.shape, BF16),
            pltpu.VMEM(inv_shared.shape, BF16),
            pltpu.VMEM((sections * mode_rows, 8 * channels), BF16),
            pltpu.VMEM((sections, mode_rows, channels), F32),
            pltpu.SemaphoreType.DMA((chunks + 3,)),
        ],
        prefetch=sec,
        flops=4 * weight_bytes,
        moved=weight_bytes,
    )
    if not packed:
        mixed = mixed.reshape(sections, devices, rows * parts, channels).transpose(1, 0, 2, 3)
        mixed = mixed.reshape(devices, sections * rows * parts, channels)
    back = exchange(mixed)
    if not packed:
        back = outer_unpack(back, sections * rows)

    field_block = (1, rows, cells, channels)
    shape3 = (rows, cells, channels)
    bias2 = bias.reshape(1, channels)
    slopes = [None] * sections
    for s in range(sections - 1, -1, -1):
        (slopes[s],) = call(
            functools.partial(slope_kernel, s, rows, packed),
            [jax.ShapeDtypeStruct(shape3, F32)],
            [
                whole(back.shape),
                pl.BlockSpec(field_block, functools.partial(lambda s, b, i: (i[0] ^ s, 0, 0, 0), s)),
                whole(synth_t.shape),
                whole(local_weight.shape),
                whole(bias2.shape),
            ],
            (back, all_states, synth_t, local_weight, bias2),
            prefetch=sec,
            flops=2 * total * cells * rows * channels,
            moved=10 * rows * cells * channels,
        )

    send_shape = (devices, rows * 8, channels) if packed else (rows, total, channels)
    turn_outs = [
        jax.ShapeDtypeStruct(shape3, BF16),
        jax.ShapeDtypeStruct(send_shape, BF16),
        jax.ShapeDtypeStruct((channels, channels), F32),
    ]

    def state_spec(s):
        return pl.BlockSpec(field_block, lambda b, i: (i[0] ^ s, 0, 0, 0))

    s = sections - 1
    carried = lax.dynamic_slice_in_dim(cotangent, section * rows, rows, 0)
    low, send, acc = call(
        functools.partial(start_kernel, packed, devices),
        turn_outs,
        [whole(shape3), whole(shape3), state_spec(s), whole(synth.shape)],
        (carried, slopes[s], all_states, synth),
        prefetch=sec,
        flops=2 * total * cells * rows * channels,
        moved=10 * rows * cells * channels,
    )
    cots = [None] * sections
    slot = channels // row_devs
    store = carried[None]
    store_shape = (sections,) + shape3
    part = mode_rows // sections

    def adjoint_scratch(*small):
        return (
            weight_scratch
            + [pltpu.VMEM(a.shape, BF16) for a in small]
            + [pltpu.VMEM((mode_rows, 16 * channels), BF16), pltpu.VMEM((mode_rows, channels), F32)]
            + [pltpu.SemaphoreType.DMA((chunks + len(small),))]
        )

    def gather_modes(values):
        split = jnp.stack(values, 0).reshape(len(values), sections, part, channels)
        mine = [lax.dynamic_index_in_dim(split, section ^ d, 1, False) for d in range(sections)]
        return [mine[0]] + [share(mine[d], d) for d in range(1, sections)]

    for s in range(sections - 1, 0, -1):
        if not packed:
            send = outer_pack(send, devices)
        got = exchange(send)
        if s == sections - 2:
            first_modes = gather_modes([coeffs[n] for n in range(sections)] + [cots[s + 1]])
            got, first_modes = lax.optimization_barrier((got, first_modes))
        got = got.reshape(grid_rows, channels)
        cots[s], inner = call(
            functools.partial(adjoint_kernel, 0),
            [
                jax.ShapeDtypeStruct((mode_rows, channels), BF16),
                jax.ShapeDtypeStruct((grid_rows, channels), BF16),
            ],
            [anywhere] * 4,
            (got, lat_shared, inv_shared, spec_weights),
            scratch=adjoint_scratch(got, lat_shared, inv_shared),
            prefetch=sec,
            flops=2 * weight_bytes,
            moved=weight_bytes,
        )
        got = exchange(inner.reshape(devices, rows * parts, channels))
        if not packed:
            got = outer_unpack(got, rows)
        last = s == 1
        first = s == sections - 1
        if last and packed:
            turn_outs[1] = jax.ShapeDtypeStruct((devices, rows * 8 + slot, channels), BF16)
        carried_at = 0 if first else s + 1
        span = 2 if last else 1
        grad_at = 0 if last else s
        store, low, send, acc = call(
            functools.partial(turn_kernel, packed, devices, row_devs, last),
            [jax.ShapeDtypeStruct(store_shape, BF16)] + turn_outs,
            [
                whole(got.shape),
                pl.BlockSpec(field_block, functools.partial(lambda n, *_: (n, 0, 0, 0), carried_at)),
                whole(shape3),
                whole(shape3),
                state_spec(s - 1),
                whole(basis.shape),
                whole(synth.shape),
                whole(local_weight.shape),
                whole(acc.shape),
            ],
            (got, store, low, slopes[s - 1], all_states, basis, synth, local_weight, acc),
            out_specs=[
                pl.BlockSpec(
                    (span,) + shape3, functools.partial(lambda n, *_: (n, 0, 0, 0), grad_at)
                )
            ]
            + [whole(o.shape) for o in turn_outs],
            prefetch=sec,
            aliases={} if first else {2: 0},
            flops=4 * total * cells * rows * channels,
            moved=16 * rows * cells * channels,
        )

    parts_of = [lax.dynamic_index_in_dim(store, section, 0, False)]
    for d in range(1, sections):
        parts_of.append(share(lax.dynamic_index_in_dim(store, section ^ d, 0, False), d))

    if not packed:
        terms = acc.reshape(row_devs, slot, channels).astype(BF16)
        terms = jnp.concatenate([terms] * sections, axis=0)
        send = jnp.concatenate([outer_pack(send, devices), terms], axis=1)
    got = exchange(send)
    inner_shape = (row_devs, grid_rows // row_devs + slot, channels)
    if not packed:
        sums = jnp.sum(got[:, rows * parts :].astype(F32), 0)
        got = got[:, : rows * parts].reshape(grid_rows, channels)
        inner_shape = (grid_rows, channels)
    cots[0], inner = call(
        functools.partial(adjoint_kernel, slot if packed else 0),
        [
            jax.ShapeDtypeStruct((mode_rows, channels), BF16),
            jax.ShapeDtypeStruct(inner_shape, BF16),
        ],
        [anywhere] * 4,
        (got, lat_shared, inv_plain, spec_weights),
        scratch=adjoint_scratch(got, lat_shared, inv_plain),
        prefetch=sec,
        flops=2 * weight_bytes,
        moved=weight_bytes,
    )
    late_modes = gather_modes(cots[:-1])
    if not packed:
        inner = inner.reshape(row_devs, grid_rows // row_devs, channels)
        both = jnp.broadcast_to(sums.astype(BF16)[None], (row_devs, slot, channels))
        inner = jnp.concatenate([inner, both], axis=1)
    got = lax.all_to_all(inner, "row", 0, 0, tiled=True)

    own_freqs = freqs // sections
    own_j = max(1, min(own_freqs, 32 // modes))
    tall = own_j * parts
    first_modes, late_modes = jnp.stack(first_modes, 0), jnp.stack(late_modes, 0)
    (d_spectral,) = call(
        functools.partial(weight_kernel, sections),
        [jax.ShapeDtypeStruct((own_freqs, row_modes, 2, channels, channels), BF16)],
        [
            pl.BlockSpec((1, m.shape[1], tall, channels), lambda a, b, i: (a, 0, b, 0))
            for m in (first_modes, late_modes)
        ],
        (first_modes, late_modes),
        grid=(sections, own_freqs // own_j),
        out_specs=[
            pl.BlockSpec(
                (own_j, modes, 2, channels, channels), lambda a, b, i: (b, i[0] ^ a, 0, 0, 0)
            )
        ],
        prefetch=sec,
        flops=8 * weight_bytes,
        moved=weight_bytes,
    )

    size = grid_rows // row_devs
    local_total = got[:, size:].reshape(channels, channels).astype(F32)
    d_local = local_total * lax.rsqrt(jnp.float32(sections * lat_cells * cells))
    if not packed:
        got = outer_unpack(got[:, :size], rows_here)
    mode_parts = [got] + [
        lax.ppermute(got, "section", [(d, 0)]) for d in range(1, sections)
    ]
    (grad_states,) = call(
        functools.partial(close_kernel, packed),
        [jax.ShapeDtypeStruct((rows_here, cells, channels), BF16)],
        [whole(shape3)] * len(parts_of) + [whole(got.shape)] * sections + [whole(basis.shape)],
        (*parts_of, *mode_parts, basis),
        grid=(sections,),
        out_specs=[pl.BlockSpec(shape3, lambda d, i: (i[0] ^ d, 0, 0))],
        prefetch=sec,
        flops=2 * total * cells * rows_here * channels,
        moved=8 * rows_here * cells * channels,
    )
    return (grad_states[None], d_spectral, d_local)


def solution(mesh):
    return jax.shard_map(
        local,
        mesh=mesh,
        in_specs=(
            P("section", "row", None, None),
            P("row", None, None),
            P(None, "row", None, None, None),
            P(),
            P(),
        ),
        out_specs=(P("section", "row", None, None), P("section", "row", None, None, None), P()),
        check_vma=False,
    )
```

```python
import functools
import math

import jax
import jax.numpy as jnp
import numpy as np
from jax import lax
from jax.experimental import pallas as pl
from jax.experimental.pallas import tpu as pltpu
from jax.sharding import PartitionSpec as P

GELU_SLOPE = math.sqrt(2.0 / math.pi)
GELU_CUBIC = 0.044715
BF16 = jnp.bfloat16
F32 = jnp.float32
ALL = ("section", "row")
VMEM_LIMIT = 63 * 1024 * 1024
CHUNK = 32


def gelu_derivative(values):
    square = values * values
    inner_arg = GELU_SLOPE * values * (1.0 + GELU_CUBIC * square)
    tangent = jnp.tanh(inner_arg)
    return 0.5 * (1.0 + tangent) + (0.5 * GELU_SLOPE) * values * (1.0 - tangent * tangent) * (
        1.0 + 3.0 * GELU_CUBIC * square
    )


def lon_tables(mode_list, lon_cells):
    phases = np.arange(lon_cells)[:, None] * mode_list[None, :] % lon_cells
    angles = phases * (2.0 * math.pi / lon_cells)
    factor = 1.0 / math.sqrt(lon_cells)
    forward = np.stack([np.cos(angles), -np.sin(angles)], 2) * factor
    doubling = np.where(mode_list == 0, 1.0, 2.0)
    backward = np.transpose(forward, (1, 2, 0)) * doubling[:, None, None]
    return (
        forward.reshape(lon_cells, -1).astype(np.float32),
        backward.reshape(-1, lon_cells).astype(np.float32),
    )


def lat_matrices(row_list, freq_count, lat_cells, modes):
    freq = np.arange(freq_count)
    signed = np.where(freq < freq_count // 2, freq, freq - freq_count)
    angles = ((signed % lat_cells)[:, None] * row_list[None, :] % lat_cells) * (
        2.0 * math.pi / lat_cells
    )
    factor = 1.0 / math.sqrt(lat_cells)
    cos, sin = np.cos(angles) * factor, np.sin(angles) * factor
    same = np.eye(modes)
    rot = np.array([[[1.0, 0.0], [0.0, 1.0]], [[0.0, 1.0], [-1.0, 0.0]]])
    block = cos[:, None, None, :, None, None] * same[None, :, None, None, :, None] * rot[0][
        None, None, :, None, None, :
    ] + sin[:, None, None, :, None, None] * same[None, :, None, None, :, None] * rot[1][
        None, None, :, None, None, :
    ]
    return block.reshape(freq_count * modes * 2, row_list.size * modes * 2).astype(np.float32)


def dot(a, b, contract=((1,), (0,))):
    return lax.dot_general(a, b, (contract, ((), ())), preferred_element_type=F32)


def unpack_rows(values, rows, packed):
    channels = values.shape[-1]
    if packed:
        devices, per_dev, _ = values.shape
        wide = values.astype(F32).reshape(devices, per_dev // 8, 8, channels)
        parts = [wide[:, r].reshape(devices * 8, channels) for r in rows]
    else:
        parts = [values[r].astype(F32) for r in rows]
    return jnp.concatenate(parts, axis=1).astype(BF16)


def pack_rows(spec, row_count, packed, devices):
    channels = spec.shape[1] // row_count
    parts = [spec[:, r * channels : (r + 1) * channels] for r in range(row_count)]
    if packed:
        parts = [p.reshape(devices, 8, channels) for p in parts]
        return jnp.concatenate(parts, axis=1).astype(BF16)
    return jnp.stack(parts, 0).astype(BF16)


def outer_pack(spec, devices):
    rows, total, channels = spec.shape
    per = total // devices
    return spec.reshape(rows, devices, per, channels).transpose(1, 0, 2, 3).reshape(
        devices, rows * per, channels
    )


def outer_unpack(received, row_count):
    devices, total, channels = received.shape
    per = total // row_count
    return received.reshape(devices, row_count, per, channels).transpose(1, 0, 2, 3).reshape(
        row_count, devices * per, channels
    )


def spectra_kernel(rows_at_once, packed, devices, fields_ref, basis_ref, out_ref):
    basis = basis_ref[...]
    row_count = fields_ref.shape[0]
    for first in range(0, row_count, rows_at_once):
        field = jnp.concatenate([fields_ref[first + r] for r in range(rows_at_once)], axis=1)
        spec = pack_rows(dot(basis, field), rows_at_once, packed, devices)
        if packed:
            out_ref[:, first * 8 : (first + rows_at_once) * 8, :] = spec
        else:
            out_ref[first : first + rows_at_once] = spec


def spread_pairs(values, per_group, sign):
    rows, _ = values.shape
    ids = lax.broadcasted_iota(jnp.int32, values.shape, 0)
    after = pltpu.roll(values, rows - 1, 0)
    before = pltpu.roll(values, 1, 0)
    turned = jnp.where(ids % 2 == 0, sign * after, -sign * before)
    pair = (ids // 2) % per_group
    parts = []
    for t in range(per_group):
        parts.append(jnp.where(pair == t, values, 0.0).astype(BF16))
        parts.append(jnp.where(pair == t, turned, 0.0).astype(BF16))
    return parts


def start_copies(sec_ref, all_ref, weights_ref, sems, early, late=()):
    chunks = sems.shape[0] - len(early) - len(late)
    span = weights_ref.shape[0] // chunks
    modes = weights_ref.shape[1]
    first = sec_ref[0] * modes

    def chunk(n):
        return pltpu.make_async_copy(
            all_ref.at[pl.ds(n * span, span), pl.ds(first, modes)],
            weights_ref.at[pl.ds(n * span, span)],
            sems.at[n],
        )

    small = [
        pltpu.make_async_copy(source, target, sems.at[chunks + n])
        for n, (source, target) in enumerate((*early, *late))
    ]
    for copy in small[: len(early)]:
        copy.start()
    for n in range(chunks):
        chunk(n).start()
    for copy in small[len(early) :]:
        copy.start()
    return chunk, chunks, small


def mix_kernel(
    steps, packed, sec_ref, x_any, lat_any, inv_any, all_ref, coeff_ref, out_ref, weights_ref,
    x_ref, lat_ref, inv_ref, lhs_ref, z_ref, sems
):
    chunk, chunks, small = start_copies(
        sec_ref, all_ref, weights_ref, sems, [(x_any, x_ref), (lat_any, lat_ref)],
        [(inv_any, inv_ref)],
    )
    small[0].wait()
    small[1].wait()
    channels = x_ref.shape[-1]
    span = x_ref.shape[0] // steps
    groups = lat_ref.shape[0] // 8
    lat = lat_ref[...]
    found = []
    for s in range(steps):
        value = dot(lat, x_ref[s * span : (s + 1) * span, :]).astype(BF16)
        coeff_ref[s] = value
        found.append(value.astype(F32).reshape(groups, 8, channels))
    tall = jnp.concatenate(found, axis=1).reshape(groups * steps * 8, channels)
    for n, part in enumerate(spread_pairs(tall, 4, -1.0)):
        lhs_ref[:, n * channels : (n + 1) * channels] = part

    block = weights_ref.shape[0] // chunks
    per_chunk = groups // chunks

    @pl.loop(0, chunks)
    def _(n):
        chunk(n).wait()
        here = weights_ref[pl.ds(n * block, block)].reshape(per_chunk, 8 * channels, channels)
        for g in range(per_chunk):
            at = pl.multiple_of((n * per_chunk + g) * (8 * steps), 8 * steps)
            mixed = dot(lhs_ref[pl.ds(at, 8 * steps), :], here[g])
            to = pl.multiple_of((n * per_chunk + g) * 8, 8)
            for s in range(steps):
                z_ref[s, pl.ds(to, 8), :] = mixed[s * 8 : (s + 1) * 8]

    small[2].wait()
    inv = inv_ref[...]
    results = [dot(inv, z_ref[s].astype(BF16)) for s in range(steps)]
    if packed:
        devices = out_ref.shape[0]
        results = [r.reshape(devices, span // devices, channels) for r in results]
        out_ref[...] = jnp.concatenate(results, axis=1).astype(BF16)
    else:
        for s in range(steps):
            out_ref[s] = results[s].astype(BF16)


def adjoint_kernel(
    extra, sec_ref, x_any, lat_any, inv_any, all_ref, coeff_ref, out_ref, weights_ref, x_ref,
    lat_ref, inv_ref, lhs_ref, z_ref, sems
):
    copies = start_copies(
        sec_ref, all_ref, weights_ref, sems, [(x_any, x_ref), (lat_any, lat_ref)],
        [(inv_any, inv_ref)],
    )
    copies[2][0].wait()
    copies[2][1].wait()
    channels = x_ref.shape[-1]
    if extra:
        wide = x_ref[...].astype(F32)
        size = wide.shape[1] - extra
        sums = jnp.sum(wide[:, size:], axis=0)
        x = wide[:, :size].reshape(-1, channels).astype(BF16)
    else:
        x = x_ref[...]
    value = dot(lat_ref[...], x).astype(BF16)
    coeff_ref[...] = value
    result = adjoint_mix(value, copies, weights_ref, inv_ref, lhs_ref, z_ref)
    if extra:
        count = out_ref.shape[0]
        result = result.reshape(count, -1, channels)
        sums = jnp.broadcast_to(sums[None], (count, extra, channels))
        result = jnp.concatenate([result, sums], axis=1)
    out_ref[...] = result.astype(BF16)


def adjoint_mix(value, copies, weights_ref, inv_ref, lhs_ref, z_ref):
    chunk, chunks, small = copies
    channels = value.shape[-1]
    groups = value.shape[0] // 16
    for n, part in enumerate(spread_pairs(value.astype(F32), 8, 1.0)):
        lhs_ref[:, n * channels : (n + 1) * channels] = part

    block = weights_ref.shape[0] // chunks
    per_chunk = groups // chunks

    @pl.loop(0, chunks)
    def _(n):
        chunk(n).wait()
        here = weights_ref[pl.ds(n * block, block)].reshape(per_chunk, 8, 2, channels, channels)
        for g in range(per_chunk):
            at = pl.multiple_of((n * per_chunk + g) * 16, 16)
            mixed = jnp.zeros((16, channels), F32)
            for t in range(8):
                left = lhs_ref[pl.ds(at, 16), 2 * t * channels : (2 * t + 2) * channels]
                right = jnp.concatenate([here[g, t, 0], here[g, t, 1]], axis=1)
                mixed = mixed + dot(left, right, ((1,), (1,)))
            z_ref[pl.ds(at, 16), :] = mixed

    small[-1].wait()
    return dot(inv_ref[...], z_ref[...].astype(BF16))


def slope_kernel(
    step, rows, packed, sec_ref, recv_ref, state_ref, synth_ref, mix_ref, bias_ref, out_ref
):
    channels = mix_ref.shape[0]
    cells = state_ref.shape[2]
    modes = unpack_rows(recv_ref[...], range(step * rows, (step + 1) * rows), packed)
    mixing = mix_ref[...]
    bias = bias_ref[...]
    tile = 256
    for w in range(0, cells, tile):
        smooth = dot(synth_ref[w : w + tile, :], modes)
        for r in range(rows):
            linear = dot(state_ref[0, r, w : w + tile, :], mixing)
            pre = smooth[:, r * channels : (r + 1) * channels] + linear + bias
            out_ref[r, w : w + tile, :] = gelu_derivative(pre)


def finish_tile(
    r, w, tile, carried, slope_ref, state_ref, low_ref
):
    low = (carried.astype(F32) * slope_ref[r, w : w + tile, :]).astype(BF16)
    low_ref[r, w : w + tile, :] = low
    term = dot(state_ref[0, r, w : w + tile, :], low, ((0,), (0,)))
    return low, term


def start_kernel(
    step, packed, devices, sec_ref, recv_ref, cot_ref, state_ref, synth_t_ref, synth_ref, mix_ref,
    bias_ref, low_ref, send_ref, acc_ref
):
    rows, cells, channels = cot_ref.shape
    modes = unpack_rows(recv_ref[...], range(step * rows, (step + 1) * rows), packed)
    mixing = mix_ref[...]
    bias = bias_ref[...]
    tile = 256
    spec, acc = None, None
    for w in range(0, cells, tile):
        smooth = dot(synth_t_ref[w : w + tile, :], modes)
        lows = []
        for r in range(rows):
            field = state_ref[0, r, w : w + tile, :]
            pre = smooth[:, r * channels : (r + 1) * channels] + dot(field, mixing) + bias
            low = cot_ref[r, w : w + tile, :].astype(F32) * gelu_derivative(pre)
            low = low.astype(BF16)
            low_ref[r, w : w + tile, :] = low
            term = dot(field, low, ((0,), (0,)))
            acc = term if acc is None else acc + term
            lows.append(low)
        part = dot(synth_ref[:, w : w + tile], jnp.concatenate(lows, axis=1))
        spec = part if spec is None else spec + part
    acc_ref[...] = acc
    send_ref[...] = pack_rows(spec, rows, packed, devices)


def gradient_tile(r, w, tile, spread, carried_ref, low_ref, mixing):
    channels = mixing.shape[0]
    linear = dot(low_ref[r, w : w + tile, :], mixing, ((1,), (1,)))
    total = (
        carried_ref[r, w : w + tile, :].astype(F32)
        + linear
        + spread[:, r * channels : (r + 1) * channels]
    )
    return total.astype(BF16)


def turn_kernel(
    packed,
    devices,
    row_devs,
    last,
    sec_ref,
    recv_ref,
    carried_ref,
    prev_ref,
    slope_ref,
    state_ref,
    basis_ref,
    synth_ref,
    mix_ref,
    acc_in_ref,
    grad_ref,
    low_ref,
    send_ref,
    acc_ref,
):
    rows, cells, channels = prev_ref.shape
    carried_ref = carried_ref.at[0]
    here = grad_ref.at[1 if last else 0]
    modes = unpack_rows(recv_ref[...], range(rows), packed)
    mixing = mix_ref[...]
    tile = 256
    spec, acc = None, acc_in_ref[...]
    for w in range(0, cells, tile):
        spread = dot(basis_ref[w : w + tile, :], modes)
        lows = []
        for r in range(rows):
            grad = gradient_tile(r, w, tile, spread, carried_ref, prev_ref, mixing)
            here[r, w : w + tile, :] = grad
            low, term = finish_tile(r, w, tile, grad, slope_ref, state_ref, low_ref)
            if last:
                base = grad.astype(F32) + dot(low, mixing, ((1,), (1,)))
                grad_ref[0, r, w : w + tile, :] = base.astype(BF16)
            lows.append(low)
            acc = acc + term
        part = dot(synth_ref[:, w : w + tile], jnp.concatenate(lows, axis=1))
        spec = part if spec is None else spec + part
    acc_ref[...] = acc
    if last and packed:
        parts = [
            spec[:, r * channels : (r + 1) * channels].reshape(devices, 8, channels)
            for r in range(rows)
        ]
        terms = acc.reshape(row_devs, channels // row_devs, channels)
        parts.append(jnp.concatenate([terms] * (devices // row_devs), axis=0))
        send_ref[...] = jnp.concatenate(parts, axis=1).astype(BF16)
    else:
        send_ref[...] = pack_rows(spec, rows, packed, devices)


def close_kernel(
    packed, sec_ref, *refs
):
    count = (len(refs) - 2) // 2
    piece_refs, mode_refs = refs[:count], refs[count : 2 * count]
    basis_ref, out_ref = refs[2 * count :]
    turn = pl.program_id(0)
    rows, cells, channels = out_ref.shape
    tile = 256

    for d in range(count):

        @pl.when((turn == d) & (sec_ref[0] != 0))
        def _():
            out_ref[...] = piece_refs[d][...]

        @pl.when((turn == d) & (sec_ref[0] == 0))
        def _():
            if packed:
                wides = [ref[...].astype(F32) for ref in mode_refs]
                modes = []
                for r in range(rows):
                    at = (d * rows + r) * 8
                    parts = [wide[:, at : at + 8].reshape(-1, channels) for wide in wides]
                    modes.append(jnp.concatenate(parts, axis=0))
                modes = jnp.concatenate(modes, axis=1).astype(BF16)
            else:
                modes = []
                for r in range(rows):
                    parts = [ref[d * rows + r].astype(F32) for ref in mode_refs]
                    modes.append(jnp.concatenate(parts, axis=0))
                modes = jnp.concatenate(modes, axis=1).astype(BF16)
            for w in range(0, cells, tile):
                spread = dot(basis_ref[w : w + tile, :], modes)
                for r in range(rows):
                    base = piece_refs[d][r, w : w + tile, :].astype(F32)
                    total = base + spread[:, r * channels : (r + 1) * channels]
                    out_ref[r, w : w + tile, :] = total.astype(BF16)


def weight_kernel(steps, sec_ref, first_ref, late_ref, out_ref):
    channels = out_ref.shape[-1]
    tall = late_ref.shape[2]
    groups = tall // 8
    lefts = [first_ref[0, s] for s in range(steps)]
    rights = [late_ref[0, s] for s in range(steps - 1)] + [first_ref[0, steps]]

    def tallied(values):
        wide = [v.astype(F32).reshape(groups, 8, channels) for v in values]
        return jnp.concatenate(wide, axis=1).reshape(groups * steps * 8, channels)

    span = steps * 8
    left, right = tallied(lefts), tallied(rights)
    ids = lax.broadcasted_iota(jnp.int32, right.shape, 0)
    turned = jnp.where(
        ids % 2 == 0,
        pltpu.roll(right, groups * span - 1, 0),
        -pltpu.roll(right, 1, 0),
    )
    right = jnp.concatenate([right, turned], axis=1).astype(BF16)
    pair = (ids // 2) % 4
    lefts = [jnp.where(pair == t, left, 0.0).astype(BF16) for t in range(4)]
    per_j = out_ref.shape[1]
    for g in range(groups):
        rhs = right[g * span : (g + 1) * span]
        for t in range(4):
            product = dot(lefts[t][g * span : (g + 1) * span], rhs, ((0,), (0,))).astype(BF16)
            j, k = divmod(g * 4 + t, per_j)
            out_ref[j, k, 0] = product[:, :channels]
            out_ref[j, k, 1] = product[:, channels:]


def whole(shape):
    return pl.BlockSpec(shape, lambda *_: (0,) * len(shape))


def call(kernel, outs, in_specs, operands, grid=(1,), out_specs=None, scratch=(), prefetch=None,
         flops=0, moved=0, aliases=None):
    if out_specs is None:
        out_specs = [whole(o.shape) for o in outs]
    count = 0 if prefetch is None else 1
    lead = () if prefetch is None else (prefetch,)
    return pl.pallas_call(
        kernel,
        out_shape=outs,
        grid_spec=pltpu.PrefetchScalarGridSpec(
            num_scalar_prefetch=count,
            grid=grid,
            in_specs=in_specs,
            out_specs=out_specs,
            scratch_shapes=list(scratch),
        ),
        input_output_aliases=aliases or {},
        compiler_params=pltpu.CompilerParams(
            vmem_limit_bytes=VMEM_LIMIT, dimension_semantics=("arbitrary",) * len(grid)
        ),
        cost_estimate=pl.CostEstimate(flops=flops, bytes_accessed=moved, transcendentals=0),
    )(*lead, *operands)


def local(states, cotangent, spec_weights, local_weight, bias):
    sections = lax.axis_size("section")
    row_devs = lax.axis_size("row")
    section = lax.axis_index("section")
    devices = sections * row_devs
    channels = local_weight.shape[0]
    cells = states.shape[2]
    rows_here = states.shape[1]
    rows = rows_here // sections
    freqs = spec_weights.shape[0]
    row_modes = spec_weights.shape[1]
    modes = row_modes // sections
    parts = 2 * modes
    lat_cells = rows_here * row_devs
    packed = parts == 8
    sec = section.astype(jnp.int32).reshape(1)

    order = (
        np.arange(row_devs)[None, :, None] * row_modes
        + np.arange(sections)[:, None, None] * modes
        + np.arange(modes)[None, None, :]
    ).reshape(-1)
    basis_np, synth_np = lon_tables(order, cells)
    basis = jnp.asarray(basis_np, BF16)
    basis_t = jnp.asarray(basis_np.T, BF16)
    synth = jnp.asarray(synth_np, BF16)
    synth_t = jnp.asarray(synth_np.T, BF16)
    row_order = (
        np.arange(row_devs)[None, :, None] * rows_here
        + np.arange(sections)[:, None, None] * rows
        + np.arange(rows)[None, None, :]
    ).reshape(-1)
    lat_plain = jnp.asarray(lat_matrices(np.arange(lat_cells), freqs, lat_cells, modes), BF16)
    shared_np = lat_matrices(row_order, freqs, lat_cells, modes)
    lat_shared = jnp.asarray(shared_np, BF16)
    inv_shared = jnp.asarray(shared_np.T, BF16)
    inv_plain = jnp.asarray(lat_matrices(np.arange(lat_cells), freqs, lat_cells, modes).T, BF16)
    mode_rows = lat_plain.shape[0]
    grid_rows = lat_plain.shape[1]

    def exchange(values):
        return lax.all_to_all(values, ALL, 0, 0, tiled=True)

    def share(piece, d):
        return lax.ppermute(piece, "section", [(i, i ^ d) for i in range(sections)])

    own = states[0].reshape(sections, rows, cells, channels)
    pieces = [lax.dynamic_index_in_dim(own, section, 0, False)]
    for d in range(1, sections):
        pieces.append(share(lax.dynamic_index_in_dim(own, section ^ d, 0, False), d))

    total = basis_t.shape[0]
    out_shape = (devices, rows_here * 8, channels) if packed else (rows_here, total, channels)
    (spectra,) = call(
        functools.partial(spectra_kernel, 2, packed, devices),
        [jax.ShapeDtypeStruct(out_shape, BF16)],
        [whole(states.shape[1:]), whole(basis_t.shape)],
        (states[0], basis_t),
        flops=2 * total * cells * rows_here * channels,
        moved=4 * rows_here * cells * channels,
    )
    if not packed:
        spectra = outer_pack(spectra, devices)
    gathered = exchange(spectra)
    near = sections - 1
    gathered, *pieces[:near] = lax.optimization_barrier((gathered, *pieces[:near]))
    gathered = gathered.reshape(sections * grid_rows, channels)
    all_states = jnp.stack(pieces[:near] + [jnp.zeros_like(pieces[0])], 0)
    all_states = lax.optimization_barrier(all_states)
    all_states = lax.dynamic_update_slice_in_dim(all_states, pieces[near][None], near, 0)

    chunk_j = max(1, min(freqs, CHUNK // modes))
    weight_scratch = [pltpu.VMEM((freqs, modes, 2, channels, channels), BF16)]
    chunks = freqs // chunk_j
    anywhere = pl.BlockSpec(memory_space=pl.ANY)
    weight_bytes = 4 * freqs * modes * channels * channels
    mixed_shape = (
        (devices, sections * rows * parts, channels)
        if packed
        else (sections, grid_rows, channels)
    )
    coeffs, mixed = call(
        functools.partial(mix_kernel, sections, packed),
        [
            jax.ShapeDtypeStruct((sections, mode_rows, channels), BF16),
            jax.ShapeDtypeStruct(mixed_shape, BF16),
        ],
        [anywhere] * 4,
        (gathered, lat_plain, inv_shared, spec_weights),
        scratch=weight_scratch
        + [
            pltpu.VMEM(gathered.shape, BF16),
            pltpu.VMEM(lat_plain.shape, BF16),
            pltpu.VMEM(inv_shared.shape, BF16),
            pltpu.VMEM((sections * mode_rows, 8 * channels), BF16),
            pltpu.VMEM((sections, mode_rows, channels), F32),
            pltpu.SemaphoreType.DMA((chunks + 3,)),
        ],
        prefetch=sec,
        flops=4 * weight_bytes,
        moved=weight_bytes,
    )
    if not packed:
        mixed = mixed.reshape(sections, devices, rows * parts, channels).transpose(1, 0, 2, 3)
        mixed = mixed.reshape(devices, sections * rows * parts, channels)
    back = exchange(mixed)
    if not packed:
        back = outer_unpack(back, sections * rows)

    field_block = (1, rows, cells, channels)
    shape3 = (rows, cells, channels)
    bias2 = bias.reshape(1, channels)
    slopes = [None] * sections
    for s in range(sections - 2, -1, -1):
        (slopes[s],) = call(
            functools.partial(slope_kernel, s, rows, packed),
            [jax.ShapeDtypeStruct(shape3, F32)],
            [
                whole(back.shape),
                pl.BlockSpec(field_block, functools.partial(lambda s, b, i: (i[0] ^ s, 0, 0, 0), s)),
                whole(synth_t.shape),
                whole(local_weight.shape),
                whole(bias2.shape),
            ],
            (back, all_states, synth_t, local_weight, bias2),
            prefetch=sec,
            flops=2 * total * cells * rows * channels,
            moved=10 * rows * cells * channels,
        )

    send_shape = (devices, rows * 8, channels) if packed else (rows, total, channels)
    turn_outs = [
        jax.ShapeDtypeStruct(shape3, BF16),
        jax.ShapeDtypeStruct(send_shape, BF16),
        jax.ShapeDtypeStruct((channels, channels), F32),
    ]

    def state_spec(s):
        return pl.BlockSpec(field_block, lambda b, i: (i[0] ^ s, 0, 0, 0))

    s = sections - 1
    carried = lax.dynamic_slice_in_dim(cotangent, section * rows, rows, 0)
    low, send, acc = call(
        functools.partial(start_kernel, s, packed, devices),
        turn_outs,
        [
            whole(back.shape),
            whole(shape3),
            state_spec(s),
            whole(synth_t.shape),
            whole(synth.shape),
            whole(local_weight.shape),
            whole(bias2.shape),
        ],
        (back, carried, all_states, synth_t, synth, local_weight, bias2),
        prefetch=sec,
        flops=2 * total * cells * rows * channels,
        moved=10 * rows * cells * channels,
    )
    cots = [None] * sections
    slot = channels // row_devs
    store = carried[None]
    store_shape = (sections,) + shape3
    part = mode_rows // sections

    def adjoint_scratch(*small):
        return (
            weight_scratch
            + [pltpu.VMEM(a.shape, BF16) for a in small]
            + [pltpu.VMEM((mode_rows, 16 * channels), BF16), pltpu.VMEM((mode_rows, channels), F32)]
            + [pltpu.SemaphoreType.DMA((chunks + len(small),))]
        )

    def gather_modes(values):
        split = jnp.stack(values, 0).reshape(len(values), sections, part, channels)
        mine = [lax.dynamic_index_in_dim(split, section ^ d, 1, False) for d in range(sections)]
        return [mine[0]] + [share(mine[d], d) for d in range(1, sections)]

    for s in range(sections - 1, 0, -1):
        if not packed:
            send = outer_pack(send, devices)
        got = exchange(send)
        if s == sections - 2:
            first_modes = gather_modes([coeffs[n] for n in range(sections)] + [cots[s + 1]])
            got, first_modes = lax.optimization_barrier((got, first_modes))
        got = got.reshape(grid_rows, channels)
        cots[s], inner = call(
            functools.partial(adjoint_kernel, 0),
            [
                jax.ShapeDtypeStruct((mode_rows, channels), BF16),
                jax.ShapeDtypeStruct((grid_rows, channels), BF16),
            ],
            [anywhere] * 4,
            (got, lat_shared, inv_shared, spec_weights),
            scratch=adjoint_scratch(got, lat_shared, inv_shared),
            prefetch=sec,
            flops=2 * weight_bytes,
            moved=weight_bytes,
        )
        got = exchange(inner.reshape(devices, rows * parts, channels))
        if not packed:
            got = outer_unpack(got, rows)
        last = s == 1
        first = s == sections - 1
        if last and packed:
            turn_outs[1] = jax.ShapeDtypeStruct((devices, rows * 8 + slot, channels), BF16)
        carried_at = 0 if first else s + 1
        span = 2 if last else 1
        grad_at = 0 if last else s
        store, low, send, acc = call(
            functools.partial(turn_kernel, packed, devices, row_devs, last),
            [jax.ShapeDtypeStruct(store_shape, BF16)] + turn_outs,
            [
                whole(got.shape),
                pl.BlockSpec(field_block, functools.partial(lambda n, *_: (n, 0, 0, 0), carried_at)),
                whole(shape3),
                whole(shape3),
                state_spec(s - 1),
                whole(basis.shape),
                whole(synth.shape),
                whole(local_weight.shape),
                whole(acc.shape),
            ],
            (got, store, low, slopes[s - 1], all_states, basis, synth, local_weight, acc),
            out_specs=[
                pl.BlockSpec(
                    (span,) + shape3, functools.partial(lambda n, *_: (n, 0, 0, 0), grad_at)
                )
            ]
            + [whole(o.shape) for o in turn_outs],
            prefetch=sec,
            aliases={} if first else {2: 0},
            flops=4 * total * cells * rows * channels,
            moved=16 * rows * cells * channels,
        )

    parts_of = [lax.dynamic_index_in_dim(store, section, 0, False)]
    for d in range(1, sections):
        parts_of.append(share(lax.dynamic_index_in_dim(store, section ^ d, 0, False), d))

    if not packed:
        terms = acc.reshape(row_devs, slot, channels).astype(BF16)
        terms = jnp.concatenate([terms] * sections, axis=0)
        send = jnp.concatenate([outer_pack(send, devices), terms], axis=1)
    got = exchange(send)
    inner_shape = (row_devs, grid_rows // row_devs + slot, channels)
    if not packed:
        sums = jnp.sum(got[:, rows * parts :].astype(F32), 0)
        got = got[:, : rows * parts].reshape(grid_rows, channels)
        inner_shape = (grid_rows, channels)
    cots[0], inner = call(
        functools.partial(adjoint_kernel, slot if packed else 0),
        [
            jax.ShapeDtypeStruct((mode_rows, channels), BF16),
            jax.ShapeDtypeStruct(inner_shape, BF16),
        ],
        [anywhere] * 4,
        (got, lat_shared, inv_plain, spec_weights),
        scratch=adjoint_scratch(got, lat_shared, inv_plain),
        prefetch=sec,
        flops=2 * weight_bytes,
        moved=weight_bytes,
    )
    late_modes = gather_modes(cots[:-1])
    if not packed:
        inner = inner.reshape(row_devs, grid_rows // row_devs, channels)
        both = jnp.broadcast_to(sums.astype(BF16)[None], (row_devs, slot, channels))
        inner = jnp.concatenate([inner, both], axis=1)
    got = lax.all_to_all(inner, "row", 0, 0, tiled=True)

    own_freqs = freqs // sections
    own_j = max(1, min(own_freqs, 32 // modes))
    tall = own_j * parts
    first_modes, late_modes = jnp.stack(first_modes, 0), jnp.stack(late_modes, 0)
    (d_spectral,) = call(
        functools.partial(weight_kernel, sections),
        [jax.ShapeDtypeStruct((own_freqs, row_modes, 2, channels, channels), BF16)],
        [
            pl.BlockSpec((1, m.shape[1], tall, channels), lambda a, b, i: (a, 0, b, 0))
            for m in (first_modes, late_modes)
        ],
        (first_modes, late_modes),
        grid=(sections, own_freqs // own_j),
        out_specs=[
            pl.BlockSpec(
                (own_j, modes, 2, channels, channels), lambda a, b, i: (b, i[0] ^ a, 0, 0, 0)
            )
        ],
        prefetch=sec,
        flops=8 * weight_bytes,
        moved=weight_bytes,
    )

    size = grid_rows // row_devs
    local_total = got[:, size:].reshape(channels, channels).astype(F32)
    d_local = local_total * lax.rsqrt(jnp.float32(sections * lat_cells * cells))
    if not packed:
        got = outer_unpack(got[:, :size], rows_here)
    mode_parts = [got] + [
        lax.ppermute(got, "section", [(d, 0)]) for d in range(1, sections)
    ]
    (grad_states,) = call(
        functools.partial(close_kernel, packed),
        [jax.ShapeDtypeStruct((rows_here, cells, channels), BF16)],
        [whole(shape3)] * len(parts_of) + [whole(got.shape)] * sections + [whole(basis.shape)],
        (*parts_of, *mode_parts, basis),
        grid=(sections,),
        out_specs=[pl.BlockSpec(shape3, lambda d, i: (i[0] ^ d, 0, 0))],
        prefetch=sec,
        flops=2 * total * cells * rows_here * channels,
        moved=8 * rows_here * cells * channels,
    )
    return (grad_states[None], d_spectral, d_local)


def solution(mesh):
    return jax.shard_map(
        local,
        mesh=mesh,
        in_specs=(
            P("section", "row", None, None),
            P("row", None, None),
            P(None, "row", None, None, None),
            P(),
            P(),
        ),
        out_specs=(P("section", "row", None, None), P("section", "row", None, None, None), P()),
        check_vma=False,
    )
```

```python
import functools
import math

import jax
import jax.numpy as jnp
import numpy as np
from jax import lax
from jax.experimental import pallas as pl
from jax.experimental.pallas import tpu as pltpu
from jax.sharding import PartitionSpec as P

GELU_SLOPE = math.sqrt(2.0 / math.pi)
GELU_CUBIC = 0.044715
BF16 = jnp.bfloat16
F32 = jnp.float32
ALL = ("section", "row")
VMEM_LIMIT = 63 * 1024 * 1024
CHUNK = 32


def gelu_derivative(values):
    square = values * values
    inner_arg = GELU_SLOPE * values * (1.0 + GELU_CUBIC * square)
    tangent = jnp.tanh(inner_arg)
    return 0.5 * (1.0 + tangent) + (0.5 * GELU_SLOPE) * values * (1.0 - tangent * tangent) * (
        1.0 + 3.0 * GELU_CUBIC * square
    )


def lon_tables(mode_list, lon_cells):
    phases = np.arange(lon_cells)[:, None] * mode_list[None, :] % lon_cells
    angles = phases * (2.0 * math.pi / lon_cells)
    factor = 1.0 / math.sqrt(lon_cells)
    forward = np.stack([np.cos(angles), -np.sin(angles)], 2) * factor
    doubling = np.where(mode_list == 0, 1.0, 2.0)
    backward = np.transpose(forward, (1, 2, 0)) * doubling[:, None, None]
    return (
        forward.reshape(lon_cells, -1).astype(np.float32),
        backward.reshape(-1, lon_cells).astype(np.float32),
    )


def lat_matrices(row_list, freq_count, lat_cells, modes):
    freq = np.arange(freq_count)
    signed = np.where(freq < freq_count // 2, freq, freq - freq_count)
    angles = ((signed % lat_cells)[:, None] * row_list[None, :] % lat_cells) * (
        2.0 * math.pi / lat_cells
    )
    factor = 1.0 / math.sqrt(lat_cells)
    cos, sin = np.cos(angles) * factor, np.sin(angles) * factor
    same = np.eye(modes)
    rot = np.array([[[1.0, 0.0], [0.0, 1.0]], [[0.0, 1.0], [-1.0, 0.0]]])
    block = cos[:, None, None, :, None, None] * same[None, :, None, None, :, None] * rot[0][
        None, None, :, None, None, :
    ] + sin[:, None, None, :, None, None] * same[None, :, None, None, :, None] * rot[1][
        None, None, :, None, None, :
    ]
    return block.reshape(freq_count * modes * 2, row_list.size * modes * 2).astype(np.float32)


def dot(a, b, contract=((1,), (0,))):
    return lax.dot_general(a, b, (contract, ((), ())), preferred_element_type=F32)


def unpack_rows(values, rows, packed):
    channels = values.shape[-1]
    if packed:
        devices, per_dev, _ = values.shape
        wide = values.astype(F32).reshape(devices, per_dev // 8, 8, channels)
        parts = [wide[:, r].reshape(devices * 8, channels) for r in rows]
    else:
        parts = [values[r].astype(F32) for r in rows]
    return jnp.concatenate(parts, axis=1).astype(BF16)


def pack_rows(spec, row_count, packed, devices):
    channels = spec.shape[1] // row_count
    parts = [spec[:, r * channels : (r + 1) * channels] for r in range(row_count)]
    if packed:
        parts = [p.reshape(devices, 8, channels) for p in parts]
        return jnp.concatenate(parts, axis=1).astype(BF16)
    return jnp.stack(parts, 0).astype(BF16)


def outer_pack(spec, devices):
    rows, total, channels = spec.shape
    per = total // devices
    return spec.reshape(rows, devices, per, channels).transpose(1, 0, 2, 3).reshape(
        devices, rows * per, channels
    )


def outer_unpack(received, row_count):
    devices, total, channels = received.shape
    per = total // row_count
    return received.reshape(devices, row_count, per, channels).transpose(1, 0, 2, 3).reshape(
        row_count, devices * per, channels
    )


def spectra_kernel(rows_at_once, packed, devices, fields_ref, basis_ref, out_ref):
    basis = basis_ref[...]
    row_count = fields_ref.shape[0]
    for first in range(0, row_count, rows_at_once):
        field = jnp.concatenate([fields_ref[first + r] for r in range(rows_at_once)], axis=1)
        spec = pack_rows(dot(basis, field), rows_at_once, packed, devices)
        if packed:
            out_ref[:, first * 8 : (first + rows_at_once) * 8, :] = spec
        else:
            out_ref[first : first + rows_at_once] = spec


def spread_pairs(values, per_group, sign):
    rows, _ = values.shape
    ids = lax.broadcasted_iota(jnp.int32, values.shape, 0)
    after = pltpu.roll(values, rows - 1, 0)
    before = pltpu.roll(values, 1, 0)
    turned = jnp.where(ids % 2 == 0, sign * after, -sign * before)
    pair = (ids // 2) % per_group
    parts = []
    for t in range(per_group):
        parts.append(jnp.where(pair == t, values, 0.0).astype(BF16))
        parts.append(jnp.where(pair == t, turned, 0.0).astype(BF16))
    return parts


def start_copies(sec_ref, all_ref, weights_ref, sems, early, late=()):
    chunks = sems.shape[0] - len(early) - len(late)
    span = weights_ref.shape[0] // chunks
    modes = weights_ref.shape[1]
    first = sec_ref[0] * modes

    def chunk(n):
        return pltpu.make_async_copy(
            all_ref.at[pl.ds(n * span, span), pl.ds(first, modes)],
            weights_ref.at[pl.ds(n * span, span)],
            sems.at[n],
        )

    small = [
        pltpu.make_async_copy(source, target, sems.at[chunks + n])
        for n, (source, target) in enumerate((*early, *late))
    ]
    for copy in small[: len(early)]:
        copy.start()
    for n in range(chunks):
        chunk(n).start()
    for copy in small[len(early) :]:
        copy.start()
    return chunk, chunks, small


def mix_kernel(
    steps, packed, sec_ref, x_any, lat_any, inv_any, all_ref, coeff_ref, out_ref, weights_ref,
    x_ref, lat_ref, inv_ref, lhs_ref, z_ref, sems
):
    chunk, chunks, small = start_copies(
        sec_ref, all_ref, weights_ref, sems, [(x_any, x_ref), (lat_any, lat_ref)],
        [(inv_any, inv_ref)],
    )
    small[0].wait()
    small[1].wait()
    channels = x_ref.shape[-1]
    span = x_ref.shape[0] // steps
    groups = lat_ref.shape[0] // 8
    lat = lat_ref[...]
    found = []
    for s in range(steps):
        value = dot(lat, x_ref[s * span : (s + 1) * span, :]).astype(BF16)
        coeff_ref[s] = value
        found.append(value.astype(F32).reshape(groups, 8, channels))
    tall = jnp.concatenate(found, axis=1).reshape(groups * steps * 8, channels)
    for n, part in enumerate(spread_pairs(tall, 4, -1.0)):
        lhs_ref[:, n * channels : (n + 1) * channels] = part

    block = weights_ref.shape[0] // chunks
    per_chunk = groups // chunks

    @pl.loop(0, chunks)
    def _(n):
        chunk(n).wait()
        here = weights_ref[pl.ds(n * block, block)].reshape(per_chunk, 8 * channels, channels)
        for g in range(per_chunk):
            at = pl.multiple_of((n * per_chunk + g) * (8 * steps), 8 * steps)
            mixed = dot(lhs_ref[pl.ds(at, 8 * steps), :], here[g])
            to = pl.multiple_of((n * per_chunk + g) * 8, 8)
            for s in range(steps):
                z_ref[s, pl.ds(to, 8), :] = mixed[s * 8 : (s + 1) * 8]

    small[2].wait()
    inv = inv_ref[...]
    results = [dot(inv, z_ref[s].astype(BF16)) for s in range(steps)]
    if packed:
        devices = out_ref.shape[0]
        results = [r.reshape(devices, span // devices, channels) for r in results]
        out_ref[...] = jnp.concatenate(results, axis=1).astype(BF16)
    else:
        for s in range(steps):
            out_ref[s] = results[s].astype(BF16)


def adjoint_kernel(
    extra, sec_ref, x_any, lat_any, inv_any, all_ref, coeff_ref, out_ref, weights_ref, x_ref,
    lat_ref, inv_ref, lhs_ref, z_ref, sems
):
    copies = start_copies(
        sec_ref, all_ref, weights_ref, sems, [(x_any, x_ref), (lat_any, lat_ref)],
        [(inv_any, inv_ref)],
    )
    copies[2][0].wait()
    copies[2][1].wait()
    channels = x_ref.shape[-1]
    if extra:
        wide = x_ref[...].astype(F32)
        size = wide.shape[1] - extra
        sums = jnp.sum(wide[:, size:], axis=0)
        x = wide[:, :size].reshape(-1, channels).astype(BF16)
    else:
        x = x_ref[...]
    value = dot(lat_ref[...], x).astype(BF16)
    coeff_ref[...] = value
    result = adjoint_mix(value, copies, weights_ref, inv_ref, lhs_ref, z_ref)
    if extra:
        count = out_ref.shape[0]
        result = result.reshape(count, -1, channels)
        sums = jnp.broadcast_to(sums[None], (count, extra, channels))
        result = jnp.concatenate([result, sums], axis=1)
    out_ref[...] = result.astype(BF16)


def adjoint_mix(value, copies, weights_ref, inv_ref, lhs_ref, z_ref):
    chunk, chunks, small = copies
    channels = value.shape[-1]
    groups = value.shape[0] // 16
    for n, part in enumerate(spread_pairs(value.astype(F32), 8, 1.0)):
        lhs_ref[:, n * channels : (n + 1) * channels] = part

    block = weights_ref.shape[0] // chunks
    per_chunk = groups // chunks

    @pl.loop(0, chunks)
    def _(n):
        chunk(n).wait()
        here = weights_ref[pl.ds(n * block, block)].reshape(per_chunk, 8, 2, channels, channels)
        for g in range(per_chunk):
            at = pl.multiple_of((n * per_chunk + g) * 16, 16)
            mixed = jnp.zeros((16, channels), F32)
            for t in range(8):
                left = lhs_ref[pl.ds(at, 16), 2 * t * channels : (2 * t + 2) * channels]
                right = jnp.concatenate([here[g, t, 0], here[g, t, 1]], axis=1)
                mixed = mixed + dot(left, right, ((1,), (1,)))
            z_ref[pl.ds(at, 16), :] = mixed

    small[-1].wait()
    return dot(inv_ref[...], z_ref[...].astype(BF16))


def slope_kernel(
    step, rows, packed, sec_ref, recv_ref, state_ref, synth_ref, mix_ref, bias_ref, out_ref
):
    channels = mix_ref.shape[0]
    cells = state_ref.shape[2]
    modes = unpack_rows(recv_ref[...], range(step * rows, (step + 1) * rows), packed)
    mixing = mix_ref[...]
    bias = bias_ref[...]
    tile = 256
    for w in range(0, cells, tile):
        smooth = dot(synth_ref[w : w + tile, :], modes)
        for r in range(rows):
            linear = dot(state_ref[0, r, w : w + tile, :], mixing)
            pre = smooth[:, r * channels : (r + 1) * channels] + linear + bias
            out_ref[r, w : w + tile, :] = gelu_derivative(pre)


def finish_tile(
    r, w, tile, carried, slope_ref, state_ref, low_ref
):
    low = (carried.astype(F32) * slope_ref[r, w : w + tile, :]).astype(BF16)
    low_ref[r, w : w + tile, :] = low
    term = dot(state_ref[0, r, w : w + tile, :], low, ((0,), (0,)))
    return low, term


def start_kernel(
    step, packed, devices, sec_ref, recv_ref, cot_ref, state_ref, synth_t_ref, synth_ref, mix_ref,
    bias_ref, low_ref, send_ref, acc_ref
):
    rows, cells, channels = cot_ref.shape
    modes = unpack_rows(recv_ref[...], range(step * rows, (step + 1) * rows), packed)
    mixing = mix_ref[...]
    bias = bias_ref[...]
    tile = 256
    spec, acc = None, None
    for w in range(0, cells, tile):
        smooth = dot(synth_t_ref[w : w + tile, :], modes)
        lows = []
        for r in range(rows):
            field = state_ref[0, r, w : w + tile, :]
            pre = smooth[:, r * channels : (r + 1) * channels] + dot(field, mixing) + bias
            low = cot_ref[r, w : w + tile, :].astype(F32) * gelu_derivative(pre)
            low = low.astype(BF16)
            low_ref[r, w : w + tile, :] = low
            term = dot(field, low, ((0,), (0,)))
            acc = term if acc is None else acc + term
            lows.append(low)
        part = dot(synth_ref[:, w : w + tile], jnp.concatenate(lows, axis=1))
        spec = part if spec is None else spec + part
    acc_ref[...] = acc
    send_ref[...] = pack_rows(spec, rows, packed, devices)


def gradient_tile(r, w, tile, spread, carried_ref, low_ref, mixing):
    channels = mixing.shape[0]
    linear = dot(low_ref[r, w : w + tile, :], mixing, ((1,), (1,)))
    total = (
        carried_ref[r, w : w + tile, :].astype(F32)
        + linear
        + spread[:, r * channels : (r + 1) * channels]
    )
    return total.astype(BF16)


def turn_kernel(
    packed,
    devices,
    row_devs,
    last,
    sec_ref,
    recv_ref,
    carried_ref,
    prev_ref,
    slope_ref,
    state_ref,
    basis_ref,
    synth_ref,
    mix_ref,
    acc_in_ref,
    grad_ref,
    low_ref,
    send_ref,
    acc_ref,
):
    rows, cells, channels = prev_ref.shape
    carried_ref = carried_ref.at[0]
    here = grad_ref.at[1 if last else 0]
    modes = unpack_rows(recv_ref[...], range(rows), packed)
    mixing = mix_ref[...]
    tile = 256
    spec, acc = None, acc_in_ref[...]
    for w in range(0, cells, tile):
        spread = dot(basis_ref[w : w + tile, :], modes)
        lows = []
        for r in range(rows):
            grad = gradient_tile(r, w, tile, spread, carried_ref, prev_ref, mixing)
            here[r, w : w + tile, :] = grad
            low, term = finish_tile(r, w, tile, grad, slope_ref, state_ref, low_ref)
            if last:
                base = grad.astype(F32) + dot(low, mixing, ((1,), (1,)))
                grad_ref[0, r, w : w + tile, :] = base.astype(BF16)
            lows.append(low)
            acc = acc + term
        part = dot(synth_ref[:, w : w + tile], jnp.concatenate(lows, axis=1))
        spec = part if spec is None else spec + part
    acc_ref[...] = acc
    if last and packed:
        parts = [
            spec[:, r * channels : (r + 1) * channels].reshape(devices, 8, channels)
            for r in range(rows)
        ]
        terms = acc.reshape(row_devs, channels // row_devs, channels)
        parts.append(jnp.concatenate([terms] * (devices // row_devs), axis=0))
        send_ref[...] = jnp.concatenate(parts, axis=1).astype(BF16)
    else:
        send_ref[...] = pack_rows(spec, rows, packed, devices)


def close_kernel(
    packed, sec_ref, *refs
):
    count = (len(refs) - 2) // 2
    piece_refs, mode_refs = refs[:count], refs[count : 2 * count]
    basis_ref, out_ref = refs[2 * count :]
    turn = pl.program_id(0)
    rows, cells, channels = out_ref.shape
    tile = 256

    for d in range(count):

        @pl.when((turn == d) & (sec_ref[0] != 0))
        def _():
            out_ref[...] = piece_refs[d][...]

        @pl.when((turn == d) & (sec_ref[0] == 0))
        def _():
            if packed:
                wides = [ref[...].astype(F32) for ref in mode_refs]
                modes = []
                for r in range(rows):
                    at = (d * rows + r) * 8
                    parts = [wide[:, at : at + 8].reshape(-1, channels) for wide in wides]
                    modes.append(jnp.concatenate(parts, axis=0))
                modes = jnp.concatenate(modes, axis=1).astype(BF16)
            else:
                modes = []
                for r in range(rows):
                    parts = [ref[d * rows + r].astype(F32) for ref in mode_refs]
                    modes.append(jnp.concatenate(parts, axis=0))
                modes = jnp.concatenate(modes, axis=1).astype(BF16)
            for w in range(0, cells, tile):
                spread = dot(basis_ref[w : w + tile, :], modes)
                for r in range(rows):
                    base = piece_refs[d][r, w : w + tile, :].astype(F32)
                    total = base + spread[:, r * channels : (r + 1) * channels]
                    out_ref[r, w : w + tile, :] = total.astype(BF16)


def weight_kernel(steps, tall, sec_ref, first_ref, late_ref, out_any, out_v, sems):
    channels = out_v.shape[-1]
    modes = out_v.shape[3]
    span_j = out_v.shape[2]
    blocks = out_v.shape[1]
    groups = tall // 8
    span = steps * 8
    block = 4 * span

    def leave(n):
        a, b = n // blocks, n % blocks
        return pltpu.make_async_copy(
            out_v.at[a, b],
            out_any.at[pl.ds(b * span_j, span_j), pl.ds((sec_ref[0] ^ a) * modes, modes)],
            sems.at[n],
        )

    def tallied(values):
        wide = [v.astype(F32).reshape(groups, 8, channels) for v in values]
        return jnp.concatenate(wide, axis=1).reshape(groups * span, channels)

    @pl.loop(0, steps * blocks)
    def _(n):
        a, b = n // blocks, n % blocks
        here = pl.ds(pl.multiple_of(b * tall, tall), tall)
        left = tallied([first_ref[a, s, here] for s in range(steps)])
        cots = [late_ref[a, s, here] for s in range(steps - 1)] + [first_ref[a, steps, here]]
        right = tallied(cots)
        ids = lax.broadcasted_iota(jnp.int32, right.shape, 0)
        turned = jnp.where(
            ids % 2 == 0,
            pltpu.roll(right, groups * span - 1, 0),
            -pltpu.roll(right, 1, 0),
        )
        right = jnp.concatenate([right, turned], axis=1).astype(BF16)
        ids = lax.broadcasted_iota(jnp.int32, (channels, block), 1)
        for first in range(0, groups, 4):
            rhs = right[first * span : first * span + block]
            turned_left = left[first * span : first * span + block].T
            for g in range(4):
                for t in range(4):
                    mine = (ids // span == g) & ((ids // 2) % 4 == t)
                    lhs = jnp.where(mine, turned_left, 0.0).astype(BF16)
                    product = dot(lhs, rhs).astype(BF16)
                    j, k = divmod((first + g) * 4 + t, modes)
                    out_v[a, b, j, k, 0] = product[:, :channels]
                    out_v[a, b, j, k, 1] = product[:, channels:]
        leave(n).start()

    @pl.loop(0, steps * blocks)
    def _(n):
        leave(n).wait()


def whole(shape):
    return pl.BlockSpec(shape, lambda *_: (0,) * len(shape))


def call(kernel, outs, in_specs, operands, grid=(1,), out_specs=None, scratch=(), prefetch=None,
         flops=0, moved=0, aliases=None):
    if out_specs is None:
        out_specs = [whole(o.shape) for o in outs]
    count = 0 if prefetch is None else 1
    lead = () if prefetch is None else (prefetch,)
    return pl.pallas_call(
        kernel,
        out_shape=outs,
        grid_spec=pltpu.PrefetchScalarGridSpec(
            num_scalar_prefetch=count,
            grid=grid,
            in_specs=in_specs,
            out_specs=out_specs,
            scratch_shapes=list(scratch),
        ),
        input_output_aliases=aliases or {},
        compiler_params=pltpu.CompilerParams(
            vmem_limit_bytes=VMEM_LIMIT, dimension_semantics=("arbitrary",) * len(grid)
        ),
        cost_estimate=pl.CostEstimate(flops=flops, bytes_accessed=moved, transcendentals=0),
    )(*lead, *operands)


def local(states, cotangent, spec_weights, local_weight, bias):
    sections = lax.axis_size("section")
    row_devs = lax.axis_size("row")
    section = lax.axis_index("section")
    devices = sections * row_devs
    channels = local_weight.shape[0]
    cells = states.shape[2]
    rows_here = states.shape[1]
    rows = rows_here // sections
    freqs = spec_weights.shape[0]
    row_modes = spec_weights.shape[1]
    modes = row_modes // sections
    parts = 2 * modes
    lat_cells = rows_here * row_devs
    packed = parts == 8
    sec = section.astype(jnp.int32).reshape(1)

    order = (
        np.arange(row_devs)[None, :, None] * row_modes
        + np.arange(sections)[:, None, None] * modes
        + np.arange(modes)[None, None, :]
    ).reshape(-1)
    basis_np, synth_np = lon_tables(order, cells)
    basis = jnp.asarray(basis_np, BF16)
    basis_t = jnp.asarray(basis_np.T, BF16)
    synth = jnp.asarray(synth_np, BF16)
    synth_t = jnp.asarray(synth_np.T, BF16)
    row_order = (
        np.arange(row_devs)[None, :, None] * rows_here
        + np.arange(sections)[:, None, None] * rows
        + np.arange(rows)[None, None, :]
    ).reshape(-1)
    lat_plain = jnp.asarray(lat_matrices(np.arange(lat_cells), freqs, lat_cells, modes), BF16)
    shared_np = lat_matrices(row_order, freqs, lat_cells, modes)
    lat_shared = jnp.asarray(shared_np, BF16)
    inv_shared = jnp.asarray(shared_np.T, BF16)
    inv_plain = jnp.asarray(lat_matrices(np.arange(lat_cells), freqs, lat_cells, modes).T, BF16)
    mode_rows = lat_plain.shape[0]
    grid_rows = lat_plain.shape[1]

    def exchange(values):
        return lax.all_to_all(values, ALL, 0, 0, tiled=True)

    def share(piece, d):
        return lax.ppermute(piece, "section", [(i, i ^ d) for i in range(sections)])

    own = states[0].reshape(sections, rows, cells, channels)
    pieces = [lax.dynamic_index_in_dim(own, section, 0, False)]
    for d in range(1, sections):
        pieces.append(share(lax.dynamic_index_in_dim(own, section ^ d, 0, False), d))

    total = basis_t.shape[0]
    out_shape = (devices, rows_here * 8, channels) if packed else (rows_here, total, channels)
    (spectra,) = call(
        functools.partial(spectra_kernel, 2, packed, devices),
        [jax.ShapeDtypeStruct(out_shape, BF16)],
        [whole(states.shape[1:]), whole(basis_t.shape)],
        (states[0], basis_t),
        flops=2 * total * cells * rows_here * channels,
        moved=4 * rows_here * cells * channels,
    )
    if not packed:
        spectra = outer_pack(spectra, devices)
    gathered = exchange(spectra)
    near = sections - 1
    gathered, *pieces[:near] = lax.optimization_barrier((gathered, *pieces[:near]))
    gathered = gathered.reshape(sections * grid_rows, channels)
    all_states = jnp.stack(pieces[:near] + [jnp.zeros_like(pieces[0])], 0)
    all_states = lax.optimization_barrier(all_states)
    all_states = lax.dynamic_update_slice_in_dim(all_states, pieces[near][None], near, 0)

    chunk_j = max(1, min(freqs, CHUNK // modes))
    weight_scratch = [pltpu.VMEM((freqs, modes, 2, channels, channels), BF16)]
    chunks = freqs // chunk_j
    anywhere = pl.BlockSpec(memory_space=pl.ANY)
    weight_bytes = 4 * freqs * modes * channels * channels
    mixed_shape = (
        (devices, sections * rows * parts, channels)
        if packed
        else (sections, grid_rows, channels)
    )
    coeffs, mixed = call(
        functools.partial(mix_kernel, sections, packed),
        [
            jax.ShapeDtypeStruct((sections, mode_rows, channels), BF16),
            jax.ShapeDtypeStruct(mixed_shape, BF16),
        ],
        [anywhere] * 4,
        (gathered, lat_plain, inv_shared, spec_weights),
        scratch=weight_scratch
        + [
            pltpu.VMEM(gathered.shape, BF16),
            pltpu.VMEM(lat_plain.shape, BF16),
            pltpu.VMEM(inv_shared.shape, BF16),
            pltpu.VMEM((sections * mode_rows, 8 * channels), BF16),
            pltpu.VMEM((sections, mode_rows, channels), F32),
            pltpu.SemaphoreType.DMA((chunks + 3,)),
        ],
        prefetch=sec,
        flops=4 * weight_bytes,
        moved=weight_bytes,
    )
    if not packed:
        mixed = mixed.reshape(sections, devices, rows * parts, channels).transpose(1, 0, 2, 3)
        mixed = mixed.reshape(devices, sections * rows * parts, channels)
    back = exchange(mixed)
    if not packed:
        back = outer_unpack(back, sections * rows)

    field_block = (1, rows, cells, channels)
    shape3 = (rows, cells, channels)
    bias2 = bias.reshape(1, channels)
    slopes = [None] * sections
    for s in range(sections - 2, -1, -1):
        (slopes[s],) = call(
            functools.partial(slope_kernel, s, rows, packed),
            [jax.ShapeDtypeStruct(shape3, F32)],
            [
                whole(back.shape),
                pl.BlockSpec(field_block, functools.partial(lambda s, b, i: (i[0] ^ s, 0, 0, 0), s)),
                whole(synth_t.shape),
                whole(local_weight.shape),
                whole(bias2.shape),
            ],
            (back, all_states, synth_t, local_weight, bias2),
            prefetch=sec,
            flops=2 * total * cells * rows * channels,
            moved=10 * rows * cells * channels,
        )

    send_shape = (devices, rows * 8, channels) if packed else (rows, total, channels)
    turn_outs = [
        jax.ShapeDtypeStruct(shape3, BF16),
        jax.ShapeDtypeStruct(send_shape, BF16),
        jax.ShapeDtypeStruct((channels, channels), F32),
    ]

    def state_spec(s):
        return pl.BlockSpec(field_block, lambda b, i: (i[0] ^ s, 0, 0, 0))

    s = sections - 1
    carried = lax.dynamic_slice_in_dim(cotangent, section * rows, rows, 0)
    low, send, acc = call(
        functools.partial(start_kernel, s, packed, devices),
        turn_outs,
        [
            whole(back.shape),
            whole(shape3),
            state_spec(s),
            whole(synth_t.shape),
            whole(synth.shape),
            whole(local_weight.shape),
            whole(bias2.shape),
        ],
        (back, carried, all_states, synth_t, synth, local_weight, bias2),
        prefetch=sec,
        flops=2 * total * cells * rows * channels,
        moved=10 * rows * cells * channels,
    )
    cots = [None] * sections
    slot = channels // row_devs
    store = carried[None]
    store_shape = (sections,) + shape3
    part = mode_rows // sections

    def adjoint_scratch(*small):
        return (
            weight_scratch
            + [pltpu.VMEM(a.shape, BF16) for a in small]
            + [pltpu.VMEM((mode_rows, 16 * channels), BF16), pltpu.VMEM((mode_rows, channels), F32)]
            + [pltpu.SemaphoreType.DMA((chunks + len(small),))]
        )

    def gather_modes(values):
        split = jnp.stack(values, 0).reshape(len(values), sections, part, channels)
        mine = [lax.dynamic_index_in_dim(split, section ^ d, 1, False) for d in range(sections)]
        return [mine[0]] + [share(mine[d], d) for d in range(1, sections)]

    for s in range(sections - 1, 0, -1):
        if not packed:
            send = outer_pack(send, devices)
        got = exchange(send)
        if s == sections - 2:
            first_modes = gather_modes([coeffs[n] for n in range(sections)] + [cots[s + 1]])
            got, first_modes = lax.optimization_barrier((got, first_modes))
        got = got.reshape(grid_rows, channels)
        cots[s], inner = call(
            functools.partial(adjoint_kernel, 0),
            [
                jax.ShapeDtypeStruct((mode_rows, channels), BF16),
                jax.ShapeDtypeStruct((grid_rows, channels), BF16),
            ],
            [anywhere] * 4,
            (got, lat_shared, inv_shared, spec_weights),
            scratch=adjoint_scratch(got, lat_shared, inv_shared),
            prefetch=sec,
            flops=2 * weight_bytes,
            moved=weight_bytes,
        )
        got = exchange(inner.reshape(devices, rows * parts, channels))
        if not packed:
            got = outer_unpack(got, rows)
        last = s == 1
        first = s == sections - 1
        if last and packed:
            turn_outs[1] = jax.ShapeDtypeStruct((devices, rows * 8 + slot, channels), BF16)
        carried_at = 0 if first else s + 1
        span = 2 if last else 1
        grad_at = 0 if last else s
        store, low, send, acc = call(
            functools.partial(turn_kernel, packed, devices, row_devs, last),
            [jax.ShapeDtypeStruct(store_shape, BF16)] + turn_outs,
            [
                whole(got.shape),
                pl.BlockSpec(field_block, functools.partial(lambda n, *_: (n, 0, 0, 0), carried_at)),
                whole(shape3),
                whole(shape3),
                state_spec(s - 1),
                whole(basis.shape),
                whole(synth.shape),
                whole(local_weight.shape),
                whole(acc.shape),
            ],
            (got, store, low, slopes[s - 1], all_states, basis, synth, local_weight, acc),
            out_specs=[
                pl.BlockSpec(
                    (span,) + shape3, functools.partial(lambda n, *_: (n, 0, 0, 0), grad_at)
                )
            ]
            + [whole(o.shape) for o in turn_outs],
            prefetch=sec,
            aliases={} if first else {2: 0},
            flops=4 * total * cells * rows * channels,
            moved=16 * rows * cells * channels,
        )

    parts_of = [lax.dynamic_index_in_dim(store, section, 0, False)]
    for d in range(1, sections):
        parts_of.append(share(lax.dynamic_index_in_dim(store, section ^ d, 0, False), d))

    if not packed:
        terms = acc.reshape(row_devs, slot, channels).astype(BF16)
        terms = jnp.concatenate([terms] * sections, axis=0)
        send = jnp.concatenate([outer_pack(send, devices), terms], axis=1)
    got = exchange(send)
    inner_shape = (row_devs, grid_rows // row_devs + slot, channels)
    if not packed:
        sums = jnp.sum(got[:, rows * parts :].astype(F32), 0)
        got = got[:, : rows * parts].reshape(grid_rows, channels)
        inner_shape = (grid_rows, channels)
    cots[0], inner = call(
        functools.partial(adjoint_kernel, slot if packed else 0),
        [
            jax.ShapeDtypeStruct((mode_rows, channels), BF16),
            jax.ShapeDtypeStruct(inner_shape, BF16),
        ],
        [anywhere] * 4,
        (got, lat_shared, inv_plain, spec_weights),
        scratch=adjoint_scratch(got, lat_shared, inv_plain),
        prefetch=sec,
        flops=2 * weight_bytes,
        moved=weight_bytes,
    )
    late_modes = gather_modes(cots[:-1])
    if not packed:
        inner = inner.reshape(row_devs, grid_rows // row_devs, channels)
        both = jnp.broadcast_to(sums.astype(BF16)[None], (row_devs, slot, channels))
        inner = jnp.concatenate([inner, both], axis=1)
    got = lax.all_to_all(inner, "row", 0, 0, tiled=True)

    own_freqs = freqs // sections
    own_j = max(1, min(own_freqs, 32 // modes))
    tall = own_j * parts
    first_modes, late_modes = jnp.stack(first_modes, 0), jnp.stack(late_modes, 0)
    blocks = own_freqs // own_j
    (d_spectral,) = call(
        functools.partial(weight_kernel, sections, tall),
        [jax.ShapeDtypeStruct((own_freqs, row_modes, 2, channels, channels), BF16)],
        [whole(first_modes.shape), whole(late_modes.shape)],
        (first_modes, late_modes),
        out_specs=[anywhere],
        scratch=[
            pltpu.VMEM((sections, blocks, own_j, modes, 2, channels, channels), BF16),
            pltpu.SemaphoreType.DMA((sections * blocks,)),
        ],
        prefetch=sec,
        flops=8 * weight_bytes,
        moved=weight_bytes,
    )

    size = grid_rows // row_devs
    local_total = got[:, size:].reshape(channels, channels).astype(F32)
    d_local = local_total * lax.rsqrt(jnp.float32(sections * lat_cells * cells))
    if not packed:
        got = outer_unpack(got[:, :size], rows_here)
    mode_parts = [got] + [
        lax.ppermute(got, "section", [(d, 0)]) for d in range(1, sections)
    ]
    (grad_states,) = call(
        functools.partial(close_kernel, packed),
        [jax.ShapeDtypeStruct((rows_here, cells, channels), BF16)],
        [whole(shape3)] * len(parts_of) + [whole(got.shape)] * sections + [whole(basis.shape)],
        (*parts_of, *mode_parts, basis),
        grid=(sections,),
        out_specs=[pl.BlockSpec(shape3, lambda d, i: (i[0] ^ d, 0, 0))],
        prefetch=sec,
        flops=2 * total * cells * rows_here * channels,
        moved=8 * rows_here * cells * channels,
    )
    return (grad_states[None], d_spectral, d_local)


def solution(mesh):
    return jax.shard_map(
        local,
        mesh=mesh,
        in_specs=(
            P("section", "row", None, None),
            P("row", None, None),
            P(None, "row", None, None, None),
            P(),
            P(),
        ),
        out_specs=(P("section", "row", None, None), P("section", "row", None, None, None), P()),
        check_vma=False,
    )
```

```python
import functools
import math

import jax
import jax.numpy as jnp
import numpy as np
from jax import lax
from jax.experimental import pallas as pl
from jax.experimental.pallas import tpu as pltpu
from jax.sharding import PartitionSpec as P

GELU_SLOPE = math.sqrt(2.0 / math.pi)
GELU_CUBIC = 0.044715
BF16 = jnp.bfloat16
F32 = jnp.float32
ALL = ("section", "row")
VMEM_LIMIT = 63 * 1024 * 1024
CHUNK = 32


def gelu_derivative(values):
    square = values * values
    inner_arg = GELU_SLOPE * values * (1.0 + GELU_CUBIC * square)
    tangent = jnp.tanh(inner_arg)
    return 0.5 * (1.0 + tangent) + (0.5 * GELU_SLOPE) * values * (1.0 - tangent * tangent) * (
        1.0 + 3.0 * GELU_CUBIC * square
    )


def lon_tables(mode_list, lon_cells):
    phases = np.arange(lon_cells)[:, None] * mode_list[None, :] % lon_cells
    angles = phases * (2.0 * math.pi / lon_cells)
    factor = 1.0 / math.sqrt(lon_cells)
    forward = np.stack([np.cos(angles), -np.sin(angles)], 2) * factor
    doubling = np.where(mode_list == 0, 1.0, 2.0)
    backward = np.transpose(forward, (1, 2, 0)) * doubling[:, None, None]
    return (
        forward.reshape(lon_cells, -1).astype(np.float32),
        backward.reshape(-1, lon_cells).astype(np.float32),
    )


def lat_matrices(row_list, freq_count, lat_cells, modes):
    freq = np.arange(freq_count)
    signed = np.where(freq < freq_count // 2, freq, freq - freq_count)
    angles = ((signed % lat_cells)[:, None] * row_list[None, :] % lat_cells) * (
        2.0 * math.pi / lat_cells
    )
    factor = 1.0 / math.sqrt(lat_cells)
    cos, sin = np.cos(angles) * factor, np.sin(angles) * factor
    same = np.eye(modes)
    rot = np.array([[[1.0, 0.0], [0.0, 1.0]], [[0.0, 1.0], [-1.0, 0.0]]])
    block = cos[:, None, None, :, None, None] * same[None, :, None, None, :, None] * rot[0][
        None, None, :, None, None, :
    ] + sin[:, None, None, :, None, None] * same[None, :, None, None, :, None] * rot[1][
        None, None, :, None, None, :
    ]
    return block.reshape(freq_count * modes * 2, row_list.size * modes * 2).astype(np.float32)


def dot(a, b, contract=((1,), (0,))):
    return lax.dot_general(a, b, (contract, ((), ())), preferred_element_type=F32)


def unpack_rows(values, rows, packed):
    channels = values.shape[-1]
    if packed:
        devices, per_dev, _ = values.shape
        wide = values.astype(F32).reshape(devices, per_dev // 8, 8, channels)
        parts = [wide[:, r].reshape(devices * 8, channels) for r in rows]
    else:
        parts = [values[r].astype(F32) for r in rows]
    return jnp.concatenate(parts, axis=1).astype(BF16)


def pack_rows(spec, row_count, packed, devices):
    channels = spec.shape[1] // row_count
    parts = [spec[:, r * channels : (r + 1) * channels] for r in range(row_count)]
    if packed:
        parts = [p.reshape(devices, 8, channels) for p in parts]
        return jnp.concatenate(parts, axis=1).astype(BF16)
    return jnp.stack(parts, 0).astype(BF16)


def outer_pack(spec, devices):
    rows, total, channels = spec.shape
    per = total // devices
    return spec.reshape(rows, devices, per, channels).transpose(1, 0, 2, 3).reshape(
        devices, rows * per, channels
    )


def outer_unpack(received, row_count):
    devices, total, channels = received.shape
    per = total // row_count
    return received.reshape(devices, row_count, per, channels).transpose(1, 0, 2, 3).reshape(
        row_count, devices * per, channels
    )


def spectra_kernel(rows_at_once, packed, devices, fields_ref, basis_ref, out_ref):
    basis = basis_ref[...]
    row_count = fields_ref.shape[0]
    for first in range(0, row_count, rows_at_once):
        field = jnp.concatenate([fields_ref[first + r] for r in range(rows_at_once)], axis=1)
        spec = pack_rows(dot(basis, field), rows_at_once, packed, devices)
        if packed:
            out_ref[:, first * 8 : (first + rows_at_once) * 8, :] = spec
        else:
            out_ref[first : first + rows_at_once] = spec


def spread_pairs(values, per_group, sign):
    rows, _ = values.shape
    ids = lax.broadcasted_iota(jnp.int32, values.shape, 0)
    after = pltpu.roll(values, rows - 1, 0)
    before = pltpu.roll(values, 1, 0)
    turned = jnp.where(ids % 2 == 0, sign * after, -sign * before)
    pair = (ids // 2) % per_group
    parts = []
    for t in range(per_group):
        parts.append(jnp.where(pair == t, values, 0.0).astype(BF16))
        parts.append(jnp.where(pair == t, turned, 0.0).astype(BF16))
    return parts


def start_copies(sec_ref, all_ref, weights_ref, sems, early, late=()):
    chunks = sems.shape[0] - len(early) - len(late)
    span = weights_ref.shape[0] // chunks
    modes = weights_ref.shape[1]
    first = sec_ref[0] * modes

    def chunk(n):
        return pltpu.make_async_copy(
            all_ref.at[pl.ds(n * span, span), pl.ds(first, modes)],
            weights_ref.at[pl.ds(n * span, span)],
            sems.at[n],
        )

    small = [
        pltpu.make_async_copy(source, target, sems.at[chunks + n])
        for n, (source, target) in enumerate((*early, *late))
    ]
    for copy in small[: len(early)]:
        copy.start()
    for n in range(chunks):
        chunk(n).start()
    for copy in small[len(early) :]:
        copy.start()
    return chunk, chunks, small


def mix_kernel(
    steps, packed, sec_ref, x_any, lat_any, inv_any, all_ref, coeff_ref, out_ref, weights_ref,
    x_ref, lat_ref, inv_ref, lhs_ref, z_ref, sems
):
    chunk, chunks, small = start_copies(
        sec_ref, all_ref, weights_ref, sems, [(x_any, x_ref), (lat_any, lat_ref)],
        [(inv_any, inv_ref)],
    )
    small[0].wait()
    small[1].wait()
    channels = x_ref.shape[-1]
    span = x_ref.shape[0] // steps
    groups = lat_ref.shape[0] // 8
    lat = lat_ref[...]
    found = []
    for s in range(steps):
        value = dot(lat, x_ref[s * span : (s + 1) * span, :]).astype(BF16)
        coeff_ref[s] = value
        found.append(value.astype(F32).reshape(groups, 8, channels))
    tall = jnp.concatenate(found, axis=1).reshape(groups * steps * 8, channels)
    for n, part in enumerate(spread_pairs(tall, 4, -1.0)):
        lhs_ref[:, n * channels : (n + 1) * channels] = part

    block = weights_ref.shape[0] // chunks
    per_chunk = groups // chunks

    @pl.loop(0, chunks)
    def _(n):
        chunk(n).wait()
        here = weights_ref[pl.ds(n * block, block)].reshape(per_chunk, 8 * channels, channels)
        for g in range(per_chunk):
            at = pl.multiple_of((n * per_chunk + g) * (8 * steps), 8 * steps)
            mixed = dot(lhs_ref[pl.ds(at, 8 * steps), :], here[g])
            to = pl.multiple_of((n * per_chunk + g) * 8, 8)
            for s in range(steps):
                z_ref[s, pl.ds(to, 8), :] = mixed[s * 8 : (s + 1) * 8]

    small[2].wait()
    inv = inv_ref[...]
    results = [dot(inv, z_ref[s].astype(BF16)) for s in range(steps)]
    if packed:
        devices = out_ref.shape[0]
        results = [r.reshape(devices, span // devices, channels) for r in results]
        out_ref[...] = jnp.concatenate(results, axis=1).astype(BF16)
    else:
        for s in range(steps):
            out_ref[s] = results[s].astype(BF16)


def adjoint_kernel(
    extra, sec_ref, x_any, lat_any, inv_any, all_ref, coeff_ref, out_ref, weights_ref, x_ref,
    lat_ref, inv_ref, lhs_ref, z_ref, sems
):
    copies = start_copies(
        sec_ref, all_ref, weights_ref, sems, [(x_any, x_ref), (lat_any, lat_ref)],
        [(inv_any, inv_ref)],
    )
    copies[2][0].wait()
    copies[2][1].wait()
    channels = x_ref.shape[-1]
    if extra:
        wide = x_ref[...].astype(F32)
        size = wide.shape[1] - extra
        sums = jnp.sum(wide[:, size:], axis=0)
        x = wide[:, :size].reshape(-1, channels).astype(BF16)
    else:
        x = x_ref[...]
    value = dot(lat_ref[...], x).astype(BF16)
    coeff_ref[...] = value
    result = adjoint_mix(value, copies, weights_ref, inv_ref, lhs_ref, z_ref)
    if extra:
        count = out_ref.shape[0]
        result = result.reshape(count, -1, channels)
        sums = jnp.broadcast_to(sums[None], (count, extra, channels))
        result = jnp.concatenate([result, sums], axis=1)
    out_ref[...] = result.astype(BF16)


def adjoint_mix(value, copies, weights_ref, inv_ref, lhs_ref, z_ref):
    chunk, chunks, small = copies
    channels = value.shape[-1]
    groups = value.shape[0] // 16
    for n, part in enumerate(spread_pairs(value.astype(F32), 8, 1.0)):
        lhs_ref[:, n * channels : (n + 1) * channels] = part

    block = weights_ref.shape[0] // chunks
    per_chunk = groups // chunks

    @pl.loop(0, chunks)
    def _(n):
        chunk(n).wait()
        here = weights_ref[pl.ds(n * block, block)].reshape(per_chunk, 8, 2, channels, channels)
        for g in range(per_chunk):
            at = pl.multiple_of((n * per_chunk + g) * 16, 16)
            mixed = jnp.zeros((16, channels), F32)
            for t in range(8):
                left = lhs_ref[pl.ds(at, 16), 2 * t * channels : (2 * t + 2) * channels]
                right = jnp.concatenate([here[g, t, 0], here[g, t, 1]], axis=1)
                mixed = mixed + dot(left, right, ((1,), (1,)))
            z_ref[pl.ds(at, 16), :] = mixed

    small[-1].wait()
    return dot(inv_ref[...], z_ref[...].astype(BF16))


def slope_kernel(
    step, rows, packed, sec_ref, recv_ref, state_ref, synth_ref, mix_ref, bias_ref, out_ref
):
    channels = mix_ref.shape[0]
    cells = state_ref.shape[2]
    modes = unpack_rows(recv_ref[...], range(step * rows, (step + 1) * rows), packed)
    mixing = mix_ref[...]
    bias = bias_ref[...]
    tile = 256
    for w in range(0, cells, tile):
        smooth = dot(synth_ref[w : w + tile, :], modes)
        for r in range(rows):
            linear = dot(state_ref[0, r, w : w + tile, :], mixing)
            pre = smooth[:, r * channels : (r + 1) * channels] + linear + bias
            out_ref[r, w : w + tile, :] = gelu_derivative(pre)


def finish_tile(
    r, w, tile, carried, slope_ref, state_ref, low_ref
):
    low = (carried.astype(F32) * slope_ref[r, w : w + tile, :]).astype(BF16)
    if low_ref is not None:
        low_ref[r, w : w + tile, :] = low
    term = dot(state_ref[0, r, w : w + tile, :], low, ((0,), (0,)))
    return low, term


def start_kernel(
    step, packed, devices, sec_ref, recv_ref, cot_ref, state_ref, synth_t_ref, synth_ref, mix_ref,
    bias_ref, low_ref, send_ref, acc_ref
):
    rows, cells, channels = cot_ref.shape
    modes = unpack_rows(recv_ref[...], range(step * rows, (step + 1) * rows), packed)
    mixing = mix_ref[...]
    bias = bias_ref[...]
    tile = 256
    spec, acc = None, None
    for w in range(0, cells, tile):
        smooth = dot(synth_t_ref[w : w + tile, :], modes)
        lows = []
        for r in range(rows):
            field = state_ref[0, r, w : w + tile, :]
            pre = smooth[:, r * channels : (r + 1) * channels] + dot(field, mixing) + bias
            low = cot_ref[r, w : w + tile, :].astype(F32) * gelu_derivative(pre)
            low = low.astype(BF16)
            low_ref[r, w : w + tile, :] = low
            term = dot(field, low, ((0,), (0,)))
            acc = term if acc is None else acc + term
            lows.append(low)
        part = dot(synth_ref[:, w : w + tile], jnp.concatenate(lows, axis=1))
        spec = part if spec is None else spec + part
    acc_ref[...] = acc
    send_ref[...] = pack_rows(spec, rows, packed, devices)


def gradient_tile(r, w, tile, spread, carried_ref, low_ref, mixing):
    channels = mixing.shape[0]
    linear = dot(low_ref[r, w : w + tile, :], mixing, ((1,), (1,)))
    total = (
        carried_ref[r, w : w + tile, :].astype(F32)
        + linear
        + spread[:, r * channels : (r + 1) * channels]
    )
    return total.astype(BF16)


def turn_kernel(
    packed,
    devices,
    row_devs,
    last,
    sec_ref,
    recv_ref,
    carried_ref,
    prev_ref,
    slope_ref,
    state_ref,
    basis_ref,
    synth_ref,
    mix_ref,
    acc_in_ref,
    grad_ref,
    *refs,
):
    low_ref = None if last else refs[0]
    send_ref, acc_ref = refs[-2:]
    rows, cells, channels = prev_ref.shape
    carried_ref = carried_ref.at[0]
    here = grad_ref.at[1 if last else 0]
    modes = unpack_rows(recv_ref[...], range(rows), packed)
    mixing = mix_ref[...]
    tile = 256
    spec, acc = None, acc_in_ref[...]
    for w in range(0, cells, tile):
        spread = dot(basis_ref[w : w + tile, :], modes)
        lows = []
        for r in range(rows):
            grad = gradient_tile(r, w, tile, spread, carried_ref, prev_ref, mixing)
            here[r, w : w + tile, :] = grad
            low, term = finish_tile(r, w, tile, grad, slope_ref, state_ref, low_ref)
            if last:
                base = grad.astype(F32) + dot(low, mixing, ((1,), (1,)))
                grad_ref[0, r, w : w + tile, :] = base.astype(BF16)
            lows.append(low)
            acc = acc + term
        part = dot(synth_ref[:, w : w + tile], jnp.concatenate(lows, axis=1))
        spec = part if spec is None else spec + part
    acc_ref[...] = acc
    if last and packed:
        parts = [
            spec[:, r * channels : (r + 1) * channels].reshape(devices, 8, channels)
            for r in range(rows)
        ]
        terms = acc.reshape(row_devs, channels // row_devs, channels)
        parts.append(jnp.concatenate([terms] * (devices // row_devs), axis=0))
        send_ref[...] = jnp.concatenate(parts, axis=1).astype(BF16)
    else:
        send_ref[...] = pack_rows(spec, rows, packed, devices)


def close_kernel(
    packed, sec_ref, *refs
):
    count = (len(refs) - 2) // 2
    piece_refs, mode_refs = refs[:count], refs[count : 2 * count]
    basis_ref, out_ref = refs[2 * count :]
    turn = pl.program_id(0)
    rows, cells, channels = out_ref.shape
    tile = 256

    for d in range(count):

        @pl.when((turn == d) & (sec_ref[0] != 0))
        def _():
            out_ref[...] = piece_refs[d][...]

        @pl.when((turn == d) & (sec_ref[0] == 0))
        def _():
            if packed:
                wides = [ref[...].astype(F32) for ref in mode_refs]
                modes = []
                for r in range(rows):
                    at = (d * rows + r) * 8
                    parts = [wide[:, at : at + 8].reshape(-1, channels) for wide in wides]
                    modes.append(jnp.concatenate(parts, axis=0))
                modes = jnp.concatenate(modes, axis=1).astype(BF16)
            else:
                modes = []
                for r in range(rows):
                    parts = [ref[d * rows + r].astype(F32) for ref in mode_refs]
                    modes.append(jnp.concatenate(parts, axis=0))
                modes = jnp.concatenate(modes, axis=1).astype(BF16)
            for w in range(0, cells, tile):
                spread = dot(basis_ref[w : w + tile, :], modes)
                for r in range(rows):
                    base = piece_refs[d][r, w : w + tile, :].astype(F32)
                    total = base + spread[:, r * channels : (r + 1) * channels]
                    out_ref[r, w : w + tile, :] = total.astype(BF16)


def weight_kernel(steps, tall, sec_ref, first_ref, late_ref, out_any, out_v, sems):
    channels = out_v.shape[-1]
    modes = out_v.shape[3]
    span_j = out_v.shape[2]
    blocks = out_v.shape[1]
    groups = tall // 8
    span = steps * 8
    block = 4 * span

    def leave(n):
        a, b = n // blocks, n % blocks
        return pltpu.make_async_copy(
            out_v.at[a, b],
            out_any.at[pl.ds(b * span_j, span_j), pl.ds((sec_ref[0] ^ a) * modes, modes)],
            sems.at[n],
        )

    def tallied(values):
        wide = [v.astype(F32).reshape(groups, 8, channels) for v in values]
        return jnp.concatenate(wide, axis=1).reshape(groups * span, channels)

    @pl.loop(0, steps * blocks)
    def _(n):
        a, b = n // blocks, n % blocks
        here = pl.ds(pl.multiple_of(b * tall, tall), tall)
        left = tallied([first_ref[a, s, here] for s in range(steps)])
        cots = [late_ref[a, s, here] for s in range(steps - 1)] + [first_ref[a, steps, here]]
        right = tallied(cots)
        ids = lax.broadcasted_iota(jnp.int32, right.shape, 0)
        turned = jnp.where(
            ids % 2 == 0,
            pltpu.roll(right, groups * span - 1, 0),
            -pltpu.roll(right, 1, 0),
        )
        right = jnp.concatenate([right, turned], axis=1).astype(BF16)
        ids = lax.broadcasted_iota(jnp.int32, (channels, block), 1)
        for first in range(0, groups, 4):
            rhs = right[first * span : first * span + block]
            turned_left = left[first * span : first * span + block].T
            for g in range(4):
                for t in range(4):
                    mine = (ids // span == g) & ((ids // 2) % 4 == t)
                    lhs = jnp.where(mine, turned_left, 0.0).astype(BF16)
                    product = dot(lhs, rhs).astype(BF16)
                    j, k = divmod((first + g) * 4 + t, modes)
                    out_v[a, b, j, k, 0] = product[:, :channels]
                    out_v[a, b, j, k, 1] = product[:, channels:]
        leave(n).start()

    @pl.loop(0, steps * blocks)
    def _(n):
        leave(n).wait()


def whole(shape):
    return pl.BlockSpec(shape, lambda *_: (0,) * len(shape))


def call(kernel, outs, in_specs, operands, grid=(1,), out_specs=None, scratch=(), prefetch=None,
         flops=0, moved=0, aliases=None):
    if out_specs is None:
        out_specs = [whole(o.shape) for o in outs]
    count = 0 if prefetch is None else 1
    lead = () if prefetch is None else (prefetch,)
    return pl.pallas_call(
        kernel,
        out_shape=outs,
        grid_spec=pltpu.PrefetchScalarGridSpec(
            num_scalar_prefetch=count,
            grid=grid,
            in_specs=in_specs,
            out_specs=out_specs,
            scratch_shapes=list(scratch),
        ),
        input_output_aliases=aliases or {},
        compiler_params=pltpu.CompilerParams(
            vmem_limit_bytes=VMEM_LIMIT, dimension_semantics=("arbitrary",) * len(grid)
        ),
        cost_estimate=pl.CostEstimate(flops=flops, bytes_accessed=moved, transcendentals=0),
    )(*lead, *operands)


def local(states, cotangent, spec_weights, local_weight, bias):
    sections = lax.axis_size("section")
    row_devs = lax.axis_size("row")
    section = lax.axis_index("section")
    devices = sections * row_devs
    channels = local_weight.shape[0]
    cells = states.shape[2]
    rows_here = states.shape[1]
    rows = rows_here // sections
    freqs = spec_weights.shape[0]
    row_modes = spec_weights.shape[1]
    modes = row_modes // sections
    parts = 2 * modes
    lat_cells = rows_here * row_devs
    packed = parts == 8
    sec = section.astype(jnp.int32).reshape(1)

    order = (
        np.arange(row_devs)[None, :, None] * row_modes
        + np.arange(sections)[:, None, None] * modes
        + np.arange(modes)[None, None, :]
    ).reshape(-1)
    basis_np, synth_np = lon_tables(order, cells)
    basis = jnp.asarray(basis_np, BF16)
    basis_t = jnp.asarray(basis_np.T, BF16)
    synth = jnp.asarray(synth_np, BF16)
    synth_t = jnp.asarray(synth_np.T, BF16)
    row_order = (
        np.arange(row_devs)[None, :, None] * rows_here
        + np.arange(sections)[:, None, None] * rows
        + np.arange(rows)[None, None, :]
    ).reshape(-1)
    lat_plain = jnp.asarray(lat_matrices(np.arange(lat_cells), freqs, lat_cells, modes), BF16)
    shared_np = lat_matrices(row_order, freqs, lat_cells, modes)
    lat_shared = jnp.asarray(shared_np, BF16)
    inv_shared = jnp.asarray(shared_np.T, BF16)
    inv_plain = jnp.asarray(lat_matrices(np.arange(lat_cells), freqs, lat_cells, modes).T, BF16)
    mode_rows = lat_plain.shape[0]
    grid_rows = lat_plain.shape[1]

    def exchange(values):
        return lax.all_to_all(values, ALL, 0, 0, tiled=True)

    def share(piece, d):
        return lax.ppermute(piece, "section", [(i, i ^ d) for i in range(sections)])

    own = states[0].reshape(sections, rows, cells, channels)
    pieces = [lax.dynamic_index_in_dim(own, section, 0, False)]
    for d in range(1, sections):
        pieces.append(share(lax.dynamic_index_in_dim(own, section ^ d, 0, False), d))

    total = basis_t.shape[0]
    out_shape = (devices, rows_here * 8, channels) if packed else (rows_here, total, channels)
    (spectra,) = call(
        functools.partial(spectra_kernel, 2, packed, devices),
        [jax.ShapeDtypeStruct(out_shape, BF16)],
        [whole(states.shape[1:]), whole(basis_t.shape)],
        (states[0], basis_t),
        flops=2 * total * cells * rows_here * channels,
        moved=4 * rows_here * cells * channels,
    )
    if not packed:
        spectra = outer_pack(spectra, devices)
    gathered = exchange(spectra)
    near = sections - 1
    gathered, *pieces[:near] = lax.optimization_barrier((gathered, *pieces[:near]))
    gathered = gathered.reshape(sections * grid_rows, channels)
    all_states = jnp.stack(pieces[:near] + [jnp.zeros_like(pieces[0])], 0)
    all_states = lax.optimization_barrier(all_states)
    all_states = lax.dynamic_update_slice_in_dim(all_states, pieces[near][None], near, 0)

    chunk_j = max(1, min(freqs, CHUNK // modes))
    weight_scratch = [pltpu.VMEM((freqs, modes, 2, channels, channels), BF16)]
    chunks = freqs // chunk_j
    anywhere = pl.BlockSpec(memory_space=pl.ANY)
    weight_bytes = 4 * freqs * modes * channels * channels
    mixed_shape = (
        (devices, sections * rows * parts, channels)
        if packed
        else (sections, grid_rows, channels)
    )
    coeffs, mixed = call(
        functools.partial(mix_kernel, sections, packed),
        [
            jax.ShapeDtypeStruct((sections, mode_rows, channels), BF16),
            jax.ShapeDtypeStruct(mixed_shape, BF16),
        ],
        [anywhere] * 4,
        (gathered, lat_plain, inv_shared, spec_weights),
        scratch=weight_scratch
        + [
            pltpu.VMEM(gathered.shape, BF16),
            pltpu.VMEM(lat_plain.shape, BF16),
            pltpu.VMEM(inv_shared.shape, BF16),
            pltpu.VMEM((sections * mode_rows, 8 * channels), BF16),
            pltpu.VMEM((sections, mode_rows, channels), F32),
            pltpu.SemaphoreType.DMA((chunks + 3,)),
        ],
        prefetch=sec,
        flops=4 * weight_bytes,
        moved=weight_bytes,
    )
    if not packed:
        mixed = mixed.reshape(sections, devices, rows * parts, channels).transpose(1, 0, 2, 3)
        mixed = mixed.reshape(devices, sections * rows * parts, channels)
    back = exchange(mixed)
    if not packed:
        back = outer_unpack(back, sections * rows)

    field_block = (1, rows, cells, channels)
    shape3 = (rows, cells, channels)
    bias2 = bias.reshape(1, channels)
    slopes = [None] * sections
    for s in range(sections - 2, -1, -1):
        (slopes[s],) = call(
            functools.partial(slope_kernel, s, rows, packed),
            [jax.ShapeDtypeStruct(shape3, F32)],
            [
                whole(back.shape),
                pl.BlockSpec(field_block, functools.partial(lambda s, b, i: (i[0] ^ s, 0, 0, 0), s)),
                whole(synth_t.shape),
                whole(local_weight.shape),
                whole(bias2.shape),
            ],
            (back, all_states, synth_t, local_weight, bias2),
            prefetch=sec,
            flops=2 * total * cells * rows * channels,
            moved=10 * rows * cells * channels,
        )

    send_shape = (devices, rows * 8, channels) if packed else (rows, total, channels)
    turn_outs = [
        jax.ShapeDtypeStruct(shape3, BF16),
        jax.ShapeDtypeStruct(send_shape, BF16),
        jax.ShapeDtypeStruct((channels, channels), F32),
    ]

    def state_spec(s):
        return pl.BlockSpec(field_block, lambda b, i: (i[0] ^ s, 0, 0, 0))

    s = sections - 1
    carried = lax.dynamic_slice_in_dim(cotangent, section * rows, rows, 0)
    low, send, acc = call(
        functools.partial(start_kernel, s, packed, devices),
        turn_outs,
        [
            whole(back.shape),
            whole(shape3),
            state_spec(s),
            whole(synth_t.shape),
            whole(synth.shape),
            whole(local_weight.shape),
            whole(bias2.shape),
        ],
        (back, carried, all_states, synth_t, synth, local_weight, bias2),
        prefetch=sec,
        flops=2 * total * cells * rows * channels,
        moved=10 * rows * cells * channels,
    )
    cots = [None] * sections
    slot = channels // row_devs
    store = carried[None]
    store_shape = (sections,) + shape3
    part = mode_rows // sections

    def adjoint_scratch(*small):
        return (
            weight_scratch
            + [pltpu.VMEM(a.shape, BF16) for a in small]
            + [pltpu.VMEM((mode_rows, 16 * channels), BF16), pltpu.VMEM((mode_rows, channels), F32)]
            + [pltpu.SemaphoreType.DMA((chunks + len(small),))]
        )

    def gather_modes(values):
        split = jnp.stack(values, 0).reshape(len(values), sections, part, channels)
        mine = [lax.dynamic_index_in_dim(split, section ^ d, 1, False) for d in range(sections)]
        return [mine[0]] + [share(mine[d], d) for d in range(1, sections)]

    for s in range(sections - 1, 0, -1):
        if not packed:
            send = outer_pack(send, devices)
        got = exchange(send)
        if s == sections - 2:
            first_modes = gather_modes([coeffs[n] for n in range(sections)] + [cots[s + 1]])
            got, first_modes = lax.optimization_barrier((got, first_modes))
        got = got.reshape(grid_rows, channels)
        cots[s], inner = call(
            functools.partial(adjoint_kernel, 0),
            [
                jax.ShapeDtypeStruct((mode_rows, channels), BF16),
                jax.ShapeDtypeStruct((grid_rows, channels), BF16),
            ],
            [anywhere] * 4,
            (got, lat_shared, inv_shared, spec_weights),
            scratch=adjoint_scratch(got, lat_shared, inv_shared),
            prefetch=sec,
            flops=2 * weight_bytes,
            moved=weight_bytes,
        )
        got = exchange(inner.reshape(devices, rows * parts, channels))
        if not packed:
            got = outer_unpack(got, rows)
        last = s == 1
        first = s == sections - 1
        if last and packed:
            turn_outs[1] = jax.ShapeDtypeStruct((devices, rows * 8 + slot, channels), BF16)
        carried_at = 0 if first else s + 1
        span = 2 if last else 1
        grad_at = 0 if last else s
        outs = turn_outs[1:] if last else turn_outs
        store, *results = call(
            functools.partial(turn_kernel, packed, devices, row_devs, last),
            [jax.ShapeDtypeStruct(store_shape, BF16)] + outs,
            [
                whole(got.shape),
                pl.BlockSpec(field_block, functools.partial(lambda n, *_: (n, 0, 0, 0), carried_at)),
                whole(shape3),
                whole(shape3),
                state_spec(s - 1),
                whole(basis.shape),
                whole(synth.shape),
                whole(local_weight.shape),
                whole(acc.shape),
            ],
            (got, store, low, slopes[s - 1], all_states, basis, synth, local_weight, acc),
            out_specs=[
                pl.BlockSpec(
                    (span,) + shape3, functools.partial(lambda n, *_: (n, 0, 0, 0), grad_at)
                )
            ]
            + [whole(o.shape) for o in outs],
            prefetch=sec,
            aliases={} if first else {2: 0},
            flops=4 * total * cells * rows * channels,
            moved=16 * rows * cells * channels,
        )
        low, send, acc = results[0], *results[-2:]

    parts_of = [lax.dynamic_index_in_dim(store, section, 0, False)]
    for d in range(1, sections):
        parts_of.append(share(lax.dynamic_index_in_dim(store, section ^ d, 0, False), d))

    if not packed:
        terms = acc.reshape(row_devs, slot, channels).astype(BF16)
        terms = jnp.concatenate([terms] * sections, axis=0)
        send = jnp.concatenate([outer_pack(send, devices), terms], axis=1)
    got = exchange(send)
    inner_shape = (row_devs, grid_rows // row_devs + slot, channels)
    if not packed:
        sums = jnp.sum(got[:, rows * parts :].astype(F32), 0)
        got = got[:, : rows * parts].reshape(grid_rows, channels)
        inner_shape = (grid_rows, channels)
    cots[0], inner = call(
        functools.partial(adjoint_kernel, slot if packed else 0),
        [
            jax.ShapeDtypeStruct((mode_rows, channels), BF16),
            jax.ShapeDtypeStruct(inner_shape, BF16),
        ],
        [anywhere] * 4,
        (got, lat_shared, inv_plain, spec_weights),
        scratch=adjoint_scratch(got, lat_shared, inv_plain),
        prefetch=sec,
        flops=2 * weight_bytes,
        moved=weight_bytes,
    )
    late_modes = gather_modes(cots[:-1])
    if not packed:
        inner = inner.reshape(row_devs, grid_rows // row_devs, channels)
        both = jnp.broadcast_to(sums.astype(BF16)[None], (row_devs, slot, channels))
        inner = jnp.concatenate([inner, both], axis=1)
    got = lax.all_to_all(inner, "row", 0, 0, tiled=True)

    own_freqs = freqs // sections
    own_j = max(1, min(own_freqs, 32 // modes))
    tall = own_j * parts
    first_modes, late_modes = jnp.stack(first_modes, 0), jnp.stack(late_modes, 0)
    blocks = own_freqs // own_j
    (d_spectral,) = call(
        functools.partial(weight_kernel, sections, tall),
        [jax.ShapeDtypeStruct((own_freqs, row_modes, 2, channels, channels), BF16)],
        [whole(first_modes.shape), whole(late_modes.shape)],
        (first_modes, late_modes),
        out_specs=[anywhere],
        scratch=[
            pltpu.VMEM((sections, blocks, own_j, modes, 2, channels, channels), BF16),
            pltpu.SemaphoreType.DMA((sections * blocks,)),
        ],
        prefetch=sec,
        flops=8 * weight_bytes,
        moved=weight_bytes,
    )

    size = grid_rows // row_devs
    local_total = got[:, size:].reshape(channels, channels).astype(F32)
    d_local = local_total * lax.rsqrt(jnp.float32(sections * lat_cells * cells))
    if not packed:
        got = outer_unpack(got[:, :size], rows_here)
    mode_parts = [got] + [
        lax.ppermute(got, "section", [(d, 0)]) for d in range(1, sections)
    ]
    (grad_states,) = call(
        functools.partial(close_kernel, packed),
        [jax.ShapeDtypeStruct((rows_here, cells, channels), BF16)],
        [whole(shape3)] * len(parts_of) + [whole(got.shape)] * sections + [whole(basis.shape)],
        (*parts_of, *mode_parts, basis),
        grid=(sections,),
        out_specs=[pl.BlockSpec(shape3, lambda d, i: (i[0] ^ d, 0, 0))],
        prefetch=sec,
        flops=2 * total * cells * rows_here * channels,
        moved=8 * rows_here * cells * channels,
    )
    return (grad_states[None], d_spectral, d_local)


def solution(mesh):
    return jax.shard_map(
        local,
        mesh=mesh,
        in_specs=(
            P("section", "row", None, None),
            P("row", None, None),
            P(None, "row", None, None, None),
            P(),
            P(),
        ),
        out_specs=(P("section", "row", None, None), P("section", "row", None, None, None), P()),
        check_vma=False,
    )
```
